256 devices in a mesh: seq: 32 (over y, z_lo, core), dp: 8 (over z_hi, x).
Axes of the slice: x: 4, y: 4, z: 8 (z_hi: 2, z_lo: 4; z = z_hi * 4 + z_lo), core: 2. Of those that a mesh axis runs over, the one named last changes fastest.
Arguments:
- query_rows: bfloat16 [16, 2048, 4096], P('dp', 'seq'), as said below
- key_rows: bfloat16 [16, 2048, 4096], P('dp', 'seq'), as said below
- value_rows: bfloat16 [16, 2048, 4096], P('dp', 'seq'), may hold values from -6 to 6
- query_tangent: bfloat16 [16, 2048, 4096], P('dp', 'seq'), may hold values from -6 to 6
- key_tangent: bfloat16 [16, 2048, 4096], P('dp', 'seq'), may hold values from -6 to 6
- value_tangent: bfloat16 [16, 2048, 4096], P('dp', 'seq'), may hold values from -6 to 6
- query_gain: float32 [4096], P('dp'), may hold values from 0.5 to 1.5
- key_gain: float32 [4096], P('dp'), may hold values from 0.5 to 1.5
Outputs:
- attended: bfloat16 [16, 2048, 4096], P('dp', 'seq')
- attended_tangent: bfloat16 [16, 2048, 4096], P('dp', 'seq')
The draws below stay inside these ranges and needn't reach their ends.
Inputs may be any that keep to these rules, and one draw needn't show every extreme that they name: `query_rows`: entries lie within -160 and 160. `key_rows`: entries lie within -160 and 160.
All inputs are finite; a program needn't handle non-finite values.
Results may differ from the reference program's by a relative error of at most 0.012.
The reference program's roundings to bfloat16 on the way (of `qn` and `dqn`) count: a program that leaves them out, or rounds other values in their place, can miss the bound.
Values may be sent and summed in bfloat16 or wider, within the bound.
A program may use at most 64 MiB of HBM per device.

```python
import jax
import jax.numpy as jnp
from jax import lax

HEADS = 32
HEAD_DIM = 128
SEQ_LEN = 2048
CLIPS = 16
WIDTH = 4096


def draw_key_rows(key, part):
    key = jax.random.fold_in(key, 7)
    return jnp.clip(jax.random.normal(key, (CLIPS, SEQ_LEN, HEADS * HEAD_DIM), jnp.float32), -4.0, 4.0).astype(jnp.bfloat16)


def draw_query_rows(key, part):
    key = jax.random.fold_in(key, 9)
    return jnp.clip(jax.random.normal(key, (CLIPS, SEQ_LEN, HEADS * HEAD_DIM), jnp.float32), -4.0, 4.0).astype(jnp.bfloat16)


def level_of(rng, dims, shards, least, top_value):
    loudness, own = 1.0, jax.random.fold_in(rng, 6)
    for dim, shards_of in shards:
        heights = jnp.exp(jax.random.uniform(jax.random.fold_in(own, dim), (shards_of,), jnp.float32, least / len(shards), top_value / len(shards)))
        loudness = loudness * jnp.repeat(heights, dims[dim] // shards_of).reshape([-1 if axis == dim else 1 for axis in range(len(dims))])
    return loudness


def noise(rng, extent, deviation, most, shards=(), dtype=jnp.bfloat16):
    entries = deviation * jax.random.normal(rng, extent, jnp.float32)
    if shards:
        entries = entries * level_of(rng, extent, shards, -0.22, 0.18)
    return jnp.clip(entries, -most, most).astype(dtype)


def setup_inputs(seed: int = 0) -> dict:
    key_list = jax.random.split(jax.random.key(seed), 9)
    query_rows = draw_query_rows(jax.random.fold_in(key_list[8], 71), 0)
    key_rows = draw_key_rows(jax.random.fold_in(key_list[8], 71), 0)
    value_rows = noise(key_list[2], (CLIPS, SEQ_LEN, WIDTH), 1.0, 6.0, ((0, 8), (1, 32)))
    query_tangent = noise(key_list[3], (CLIPS, SEQ_LEN, WIDTH), 1.0, 6.0, ((0, 8), (1, 32)))
    key_tangent = noise(key_list[4], (CLIPS, SEQ_LEN, WIDTH), 1.0, 6.0, ((0, 8), (1, 32)))
    value_tangent = noise(key_list[5], (CLIPS, SEQ_LEN, WIDTH), 1.0, 6.0, ((0, 8), (1, 32)))
    query_gain = jnp.clip(0.5 + 1.0 * jax.random.uniform(key_list[6], (WIDTH,), jnp.float32) ** level_of(key_list[6], (WIDTH,), ((0, 8),), -0.2, 0.2), 0.5, 1.5)
    key_gain = jnp.clip(0.5 + 1.0 * jax.random.uniform(key_list[7], (WIDTH,), jnp.float32) ** level_of(key_list[7], (WIDTH,), ((0, 8),), -0.2, 0.2), 0.5, 1.5)
    return dict(query_rows=query_rows, key_rows=key_rows, value_rows=value_rows, query_tangent=query_tangent, key_tangent=key_tangent, value_tangent=value_tangent, query_gain=query_gain, key_gain=key_gain)


EPS = 1e-06

def normalize(rows, tangent, gain):
    xf = rows.astype(jnp.float32)
    dxf = tangent.astype(jnp.float32)
    inverse = lax.rsqrt(lax.optimization_barrier(jnp.mean(xf * xf, axis=-1, keepdims=True)) + EPS)
    cross = lax.optimization_barrier(jnp.mean(xf * dxf, axis=-1, keepdims=True))
    normed = xf * inverse * gain
    dnormed = (dxf * inverse - xf * inverse ** 3 * cross) * gain
    return (normed.astype(jnp.bfloat16), dnormed.astype(jnp.bfloat16))

def head_attention(parts):
    qh, kh, vh, dqh, dkh, dvh = parts
    length, hdim = qh.shape
    block = min(512, length)
    scale = hdim ** (-0.5)

    def one_block(pair):
        qblock, dqblock = pair
        scores = jnp.dot(qblock, kh.T, preferred_element_type=jnp.float32) * scale
        top = lax.optimization_barrier(jnp.max(scores, axis=-1, keepdims=True))
        weights = jnp.exp(scores - top)
        weights = weights / lax.optimization_barrier(jnp.sum(weights, axis=-1, keepdims=True))
        tangent = (jnp.dot(dqblock, kh.T, preferred_element_type=jnp.float32) + jnp.dot(qblock, dkh.T, preferred_element_type=jnp.float32)) * scale
        dweights = weights * (tangent - lax.optimization_barrier(jnp.sum(weights * tangent, axis=-1, keepdims=True)))
        weights_low = weights.astype(jnp.bfloat16)
        tangent_low = dweights.astype(jnp.bfloat16)
        output = jnp.dot(weights_low, vh, preferred_element_type=jnp.float32).astype(jnp.bfloat16)
        doutput = (jnp.dot(tangent_low, vh, preferred_element_type=jnp.float32) + jnp.dot(weights_low, dvh, preferred_element_type=jnp.float32)).astype(jnp.bfloat16)
        return (output, doutput)
    blocks = length // block
    output, doutput = lax.map(one_block, (qh.reshape(blocks, block, hdim), dqh.reshape(blocks, block, hdim)))
    return (output.reshape(length, hdim), doutput.reshape(length, hdim))

def reference(query_rows, key_rows, value_rows, query_tangent, key_tangent, value_tangent, query_gain, key_gain):
    qn, dqn = normalize(query_rows, query_tangent, query_gain)
    kn, dkn = normalize(key_rows, key_tangent, key_gain)

    def split(array):
        return array.reshape(CLIPS, SEQ_LEN, HEADS, HEAD_DIM).transpose(0, 2, 1, 3).reshape(CLIPS * HEADS, SEQ_LEN, HEAD_DIM)

    def join(array):
        return array.reshape(CLIPS, HEADS, SEQ_LEN, HEAD_DIM).transpose(0, 2, 1, 3).reshape(CLIPS, SEQ_LEN, WIDTH)
    output, doutput = lax.map(head_attention, (split(qn), split(kn), split(value_rows), split(dqn), split(dkn), split(value_tangent)))
    return (join(output), join(doutput))
```

```python
import jax
import jax.numpy as jnp
from jax import lax
from jax.experimental import pallas as pl
from jax.experimental.pallas import tpu as pltpu
from jax.sharding import PartitionSpec as P

EPS = 1e-06
DIM = 128
TILE = 256
MESH = pl.DeviceIdType.MESH
NT = (((1,), (1,)), ((), ()))
V, DV, K, DK, Q, DQ = range(6)


def attend(query, dquery, key, dkey, value, dvalue):
    scale = DIM**-0.5
    scores = lax.dot_general(query, key, NT, preferred_element_type=jnp.float32) * scale
    weights = jnp.exp(scores - jnp.max(scores, axis=-1, keepdims=True))
    weights = weights * (1.0 / jnp.sum(weights, axis=-1, keepdims=True))
    tangent = (
        lax.dot_general(
            jnp.concatenate([dquery, query], 1),
            jnp.concatenate([key, dkey], 1),
            NT,
            preferred_element_type=jnp.float32,
        )
        * scale
    )
    mean = jnp.sum(weights * tangent, axis=-1, keepdims=True)
    low = weights.astype(jnp.bfloat16)
    dlow = (weights * (tangent - mean)).astype(jnp.bfloat16)
    both = jnp.dot(low, jnp.concatenate([value, dvalue], 1), preferred_element_type=jnp.float32)
    dout = jnp.dot(dlow, value, preferred_element_type=jnp.float32) + both[:, DIM:]
    return both[:, :DIM].astype(jnp.bfloat16), dout.astype(jnp.bfloat16)


def make_kernel(seq, dp, clips, rows, width):
    per_tile = TILE // rows
    tiles = seq // per_tile

    def kernel(
        q_ref,
        k_ref,
        v_ref,
        dq_ref,
        dk_ref,
        dv_ref,
        gq_ref,
        gk_ref,
        o_ref,
        do_ref,
        normed,
        gathered,
        gains,
        held,
        results,
        load_sem,
        gain_send,
        gain_recv,
        send_sem,
        recv_sem,
        back_send,
        back_recv,
        own_sem,
        own_back,
    ):
        me = lax.axis_index("seq")
        group = lax.axis_index("dp")
        barrier = pltpu.get_barrier_semaphore()

        def greet_seq(r, carry):
            peer = lax.rem(me + r, seq)
            pl.semaphore_signal(barrier, inc=1, device_id={"seq": peer}, device_id_type=MESH)
            return carry

        def greet_dp(r, carry):
            peer = lax.rem(group + r, dp)
            pl.semaphore_signal(barrier, inc=1, device_id={"dp": peer}, device_id_type=MESH)
            return carry

        lax.fori_loop(1, dp, greet_dp, 0)
        lax.fori_loop(1, seq, greet_seq, 0)

        sources = {K: k_ref, DK: dk_ref, Q: q_ref, DQ: dq_ref}
        loads = [
            pltpu.make_async_copy(ref, normed.at[slot - K], load_sem.at[slot - K])
            for slot, ref in sources.items()
        ]
        gain_loads = [
            pltpu.make_async_copy(ref, gathered.at[which, group], load_sem.at[4 + which])
            for which, ref in enumerate((gq_ref, gk_ref))
        ]
        for copy in gain_loads + loads:
            copy.start()
        pl.semaphore_wait(barrier, seq + dp - 2)

        for which, ref in enumerate((gq_ref, gk_ref)):

            def send_gain(r, carry):
                peer = lax.rem(group + r, dp)
                pltpu.make_async_remote_copy(
                    src_ref=ref,
                    dst_ref=gathered.at[which, group],
                    send_sem=gain_send.at[which],
                    recv_sem=gain_recv.at[which],
                    device_id={"dp": peer},
                    device_id_type=MESH,
                ).start()
                return carry

            lax.fori_loop(1, dp, send_gain, 0)

        def source(clip, slot, head):
            columns = pl.ds(pl.multiple_of(head * DIM, DIM), DIM)
            if slot == V:
                return v_ref.at[clip, :, columns]
            if slot == DV:
                return dv_ref.at[clip, :, columns]
            return normed.at[slot - K, clip, :, columns]

        def send(clip, slot):
            def one(r, carry):
                head = lax.rem(me + r, seq)
                pltpu.make_async_remote_copy(
                    src_ref=source(clip, slot, head),
                    dst_ref=held.at[clip, slot, me],
                    send_sem=send_sem.at[clip, slot],
                    recv_sem=recv_sem.at[clip, slot],
                    device_id={"seq": head},
                    device_id_type=MESH,
                ).start()
                return carry

            lax.fori_loop(1, seq, one, 0)
            pltpu.make_async_copy(
                source(clip, slot, me), held.at[clip, slot, me], own_sem.at[clip, slot]
            ).start()

        def others(clip, slot):
            return held.at[clip, slot, pl.ds(0, seq - 1)]

        def arrive(clip, slot):
            pltpu.make_async_copy(
                others(clip, slot), others(clip, slot), recv_sem.at[clip, slot]
            ).wait()
            pltpu.make_async_copy(
                held.at[clip, slot, me], held.at[clip, slot, me], own_sem.at[clip, slot]
            ).wait()

        def normalize(clip, slot, which):
            def step(i, carry):
                part = pl.ds(pl.multiple_of(i * 16, 16), 16)
                x = normed[slot - K, clip, part, :].astype(jnp.float32)
                dx = normed[slot + 1 - K, clip, part, :].astype(jnp.float32)
                gain = gains[which]
                inverse = lax.rsqrt(jnp.sum(x * x, axis=-1, keepdims=True) * (1.0 / width) + EPS)
                cross = jnp.sum(x * dx, axis=-1, keepdims=True) * (1.0 / width)
                normed[slot - K, clip, part, :] = (x * inverse * gain).astype(jnp.bfloat16)
                normed[slot + 1 - K, clip, part, :] = (
                    (dx * inverse - x * (inverse * inverse * inverse * cross)) * gain
                ).astype(jnp.bfloat16)
                return carry

            lax.fori_loop(0, rows // 16, step, 0)

        send(0, V)
        send(0, DV)

        for which in range(2):
            gain_loads[which].wait()
            other = gathered.at[which, pl.ds(0, dp - 1)]
            pltpu.make_async_copy(other, other, gain_recv.at[which]).wait()
            chunks = width // dp // DIM
            for owner in range(dp):
                for j in range(chunks):
                    at = (owner * chunks + j) * DIM
                    gains[which, :, at : at + DIM] = gathered[which, owner, j : j + 1, :]
        for copy in loads:
            copy.wait()

        normalize(0, K, 1)
        send(0, K)
        send(0, DK)
        normalize(0, Q, 0)
        send(0, Q)
        send(0, DQ)
        for clip in range(1, clips):
            normalize(clip, K, 1)
            normalize(clip, Q, 0)

        chip_row, half = me // 8, (me % 8) // 4

        def tile_of(i):
            crosses = 1 - i // (tiles // 2)
            row = lax.rem(chip_row + i % (tiles // 2), tiles // 2)
            return row * 2 + (half + crosses) % 2

        def compute(clip, i):
            first = tile_of(i) * per_tile
            took = pl.ds(first, per_tile)

            def whole(slot):
                return held[clip, slot].reshape(seq * rows, DIM)

            out, dout = attend(
                held[clip, Q, took].reshape(TILE, DIM),
                held[clip, DQ, took].reshape(TILE, DIM),
                whole(K),
                whole(DK),
                whole(V),
                whole(DV),
            )
            results[clip, 0, took] = out.reshape(per_tile, rows, DIM)
            results[clip, 1, took] = dout.reshape(per_tile, rows, DIM)

        mine = pl.ds(pl.multiple_of(me * DIM, DIM), DIM)

        def give_back(clip, which, i):
            ref = (o_ref, do_ref)[which]
            first = tile_of(i) * per_tile
            for r in range(per_tile):
                token = first + r

                @pl.when(token != me)
                def _():
                    pltpu.make_async_remote_copy(
                        src_ref=results.at[clip, which, token],
                        dst_ref=ref.at[clip, :, mine],
                        send_sem=back_send.at[clip, which],
                        recv_sem=back_recv.at[clip, which],
                        device_id={"seq": token},
                        device_id_type=MESH,
                    ).start()

                @pl.when(token == me)
                def _():
                    pltpu.make_async_copy(
                        results.at[clip, which, token],
                        ref.at[clip, :, mine],
                        own_back.at[clip, which],
                    ).start()

        def loop(low, high, body):
            def step(i, carry):
                body(i)
                return carry

            lax.fori_loop(low, high, step, 0)

        send(1, V)
        arrive(0, V)
        send(1, DV)
        arrive(0, DV)
        send(1, K)
        arrive(0, K)
        arrive(0, DK)
        arrive(0, Q)
        arrive(0, DQ)
        send(1, DK)
        loop(0, 3, lambda i: compute(0, i))
        arrive(1, V)
        send(1, Q)
        loop(3, 6, lambda i: compute(0, i))
        arrive(1, DV)
        send(1, DQ)
        loop(6, tiles, lambda i: compute(0, i))
        arrive(1, K)
        arrive(1, DK)
        loop(0, tiles, lambda i: give_back(0, 0, i))
        arrive(1, Q)
        loop(0, tiles, lambda i: give_back(0, 1, i))
        arrive(1, DQ)

        def last(i):
            compute(1, i)
            give_back(1, 0, i)
            give_back(1, 1, i)

        loop(0, tiles, last)

        for which in range(2):
            other = gathered.at[which, pl.ds(0, dp - 1)]
            pltpu.make_async_copy(other, other, gain_send.at[which]).wait()
        for clip in range(clips):
            for slot in range(6):
                pltpu.make_async_copy(
                    others(clip, slot), others(clip, slot), send_sem.at[clip, slot]
                ).wait()
            for which in range(2):
                own, some = results.at[clip, which, 0], results.at[clip, which, pl.ds(0, seq - 1)]
                pltpu.make_async_copy(some, some, back_send.at[clip, which]).wait()
                pltpu.make_async_copy(own, own, own_back.at[clip, which]).wait()
                pltpu.make_async_copy(some, some, back_recv.at[clip, which]).wait()

    return kernel


def solution(mesh):
    seq, dp = mesh.shape["seq"], mesh.shape["dp"]

    def on_device(q, k, v, dq, dk, dv, gq, gk):
        clips, rows, width = q.shape
        gq, gk = (gain.reshape(gain.shape[0] // DIM, DIM) for gain in (gq, gk))
        out = jax.ShapeDtypeStruct(q.shape, q.dtype)
        pieces = clips * seq * seq * rows
        return pl.pallas_call(
            make_kernel(seq, dp, clips, rows, width),
            out_shape=(out, out),
            in_specs=[pl.BlockSpec(memory_space=pl.ANY)] * 8,
            out_specs=(pl.BlockSpec(memory_space=pl.ANY),) * 2,
            scratch_shapes=[
                pltpu.VMEM((4, clips, rows, width), jnp.bfloat16),
                pltpu.VMEM((2, dp) + gq.shape, jnp.float32),
                pltpu.VMEM((2, 1, width), jnp.float32),
                pltpu.VMEM((clips, 6, seq, rows, DIM), jnp.bfloat16),
                pltpu.VMEM((clips, 2, seq, rows, DIM), jnp.bfloat16),
                pltpu.SemaphoreType.DMA((6,)),
                pltpu.SemaphoreType.DMA((2,)),
                pltpu.SemaphoreType.DMA((2,)),
                pltpu.SemaphoreType.DMA((clips, 6)),
                pltpu.SemaphoreType.DMA((clips, 6)),
                pltpu.SemaphoreType.DMA((clips, 2)),
                pltpu.SemaphoreType.DMA((clips, 2)),
                pltpu.SemaphoreType.DMA((clips, 6)),
                pltpu.SemaphoreType.DMA((clips, 2)),
            ],
            compiler_params=pltpu.CompilerParams(
                collective_id=0, has_side_effects=True, vmem_limit_bytes=56 * 2**20
            ),
            cost_estimate=pl.CostEstimate(
                flops=12 * pieces * seq * rows * DIM // seq,
                bytes_accessed=8 * 2 * clips * rows * width,
                transcendentals=pieces * seq * rows // seq,
            ),
        )(q, k, v, dq, dk, dv, gq, gk)

    shard = P("dp", "seq", None)
    return jax.shard_map(
        on_device,
        mesh=mesh,
        in_specs=(shard,) * 6 + (P("dp"),) * 2,
        out_specs=(shard, shard),
        check_vma=False,
    )
```

```python
import jax
import jax.numpy as jnp
from jax import lax
from jax.experimental import pallas as pl
from jax.experimental.pallas import tpu as pltpu
from jax.sharding import PartitionSpec as P

EPS = 1e-06
DIM = 128
TILE = 256
MESH = pl.DeviceIdType.MESH
NT = (((1,), (1,)), ((), ()))
V, DV, K, DK, Q, DQ = range(6)


def attend(query, dquery, key, dkey, value, dvalue):
    scale = DIM**-0.5
    scores = lax.dot_general(query, key, NT, preferred_element_type=jnp.float32) * scale
    weights = jnp.exp(scores - jnp.max(scores, axis=-1, keepdims=True))
    weights = weights * (1.0 / jnp.sum(weights, axis=-1, keepdims=True))
    tangent = (
        lax.dot_general(
            jnp.concatenate([dquery, query], 1),
            jnp.concatenate([key, dkey], 1),
            NT,
            preferred_element_type=jnp.float32,
        )
        * scale
    )
    mean = jnp.sum(weights * tangent, axis=-1, keepdims=True)
    low = weights.astype(jnp.bfloat16)
    dlow = (weights * (tangent - mean)).astype(jnp.bfloat16)
    both = jnp.dot(low, jnp.concatenate([value, dvalue], 1), preferred_element_type=jnp.float32)
    dout = jnp.dot(dlow, value, preferred_element_type=jnp.float32) + both[:, DIM:]
    return both[:, :DIM].astype(jnp.bfloat16), dout.astype(jnp.bfloat16)


def write_out(a_ref, b_ref, o_ref, do_ref, sem):
    copies = [
        pltpu.make_async_copy(a_ref, o_ref, sem.at[0]),
        pltpu.make_async_copy(b_ref, do_ref, sem.at[1]),
    ]
    for copy in copies:
        copy.start()
    for copy in copies:
        copy.wait()


def make_kernel(seq, dp, clips, rows, width):
    per_tile = TILE // rows
    plane = 8
    tiles = seq // per_tile

    def kernel(
        q_ref,
        k_ref,
        v_ref,
        dq_ref,
        dk_ref,
        dv_ref,
        gq_ref,
        gk_ref,
        o_ref,
        do_ref,
        normed,
        gathered,
        gains,
        held,
        results,
        load_sem,
        gain_send,
        gain_recv,
        hand_send,
        hand_recv,
        entered,
        send_sem,
        recv_sem,
        back_send,
        back_recv,
        own_sem,
        own_back,
    ):
        me = lax.axis_index("seq")
        group = lax.axis_index("dp")
        gate = jnp.logical_and(me // plane == 0, me % 2 == 0)
        beside = jnp.logical_and(me // plane == 0, me % 2 == 1)
        barrier = pltpu.get_barrier_semaphore()

        def greet_seq(r, carry):
            peer = lax.rem(me + r, seq)

            @pl.when(jnp.logical_or(peer // plane > 0, peer % 2 == 1))
            def _():
                pl.semaphore_signal(barrier, inc=1, device_id={"seq": peer}, device_id_type=MESH)

            return carry

        def greet_dp(r, carry):
            peer = lax.rem(group + r, dp)
            pl.semaphore_signal(barrier, inc=1, device_id={"dp": peer}, device_id_type=MESH)
            return carry

        lax.fori_loop(1, seq, greet_seq, 0)

        @pl.when(gate)
        def _():
            lax.fori_loop(1, dp, greet_dp, 0)

        sources = {K: k_ref, DK: dk_ref, Q: q_ref, DQ: dq_ref}
        loads = [
            pltpu.make_async_copy(ref, normed.at[slot - K], load_sem.at[slot - K])
            for slot, ref in sources.items()
        ]
        for copy in loads:
            copy.start()

        @pl.when(jnp.logical_not(gate))
        def _():
            pl.semaphore_wait(barrier, seq - 1)

        @pl.when(beside)
        def _():
            pl.semaphore_signal(entered, inc=1, device_id={"seq": me - 1}, device_id_type=MESH)

        @pl.when(gate)
        def _():
            pl.semaphore_wait(entered, 1)

        def exchange_gains():
            gain_loads = [
                pltpu.make_async_copy(ref, gathered.at[which, group], load_sem.at[4 + which])
                for which, ref in enumerate((gq_ref, gk_ref))
            ]
            for copy in gain_loads:
                copy.start()
            pl.semaphore_wait(barrier, dp - 1)
            for which, ref in enumerate((gq_ref, gk_ref)):

                def send_gain(r, carry):
                    peer = lax.rem(group + r, dp)
                    pltpu.make_async_remote_copy(
                        src_ref=ref,
                        dst_ref=gathered.at[which, group],
                        send_sem=gain_send.at[which],
                        recv_sem=gain_recv.at[which],
                        device_id={"dp": peer},
                        device_id_type=MESH,
                    ).start()
                    return carry

                lax.fori_loop(1, dp, send_gain, 0)
            for which in range(2):
                gain_loads[which].wait()
                other = gathered.at[which, pl.ds(0, dp - 1)]
                pltpu.make_async_copy(other, other, gain_recv.at[which]).wait()

            def hand_on(r, carry):
                peer = me + lax.rem(r, 2) + r // 2 * plane
                pltpu.make_async_remote_copy(
                    src_ref=gathered,
                    dst_ref=gathered,
                    send_sem=hand_send.at[r],
                    recv_sem=hand_recv,
                    device_id={"seq": peer},
                    device_id_type=MESH,
                ).start()
                return carry

            lax.fori_loop(1, seq // plane * 2, hand_on, 0)

        def source(clip, slot, head):
            columns = pl.ds(pl.multiple_of(head * DIM, DIM), DIM)
            if slot == V:
                return v_ref.at[clip, :, columns]
            if slot == DV:
                return dv_ref.at[clip, :, columns]
            return normed.at[slot - K, clip, :, columns]

        def send(clip, slot):
            def one(r, carry):
                head = lax.rem(me + r, seq)
                pltpu.make_async_remote_copy(
                    src_ref=source(clip, slot, head),
                    dst_ref=held.at[clip, slot, me],
                    send_sem=send_sem.at[clip, slot],
                    recv_sem=recv_sem.at[clip, slot],
                    device_id={"seq": head},
                    device_id_type=MESH,
                ).start()
                return carry

            lax.fori_loop(1, seq, one, 0)
            pltpu.make_async_copy(
                source(clip, slot, me), held.at[clip, slot, me], own_sem.at[clip, slot]
            ).start()

        def others(clip, slot):
            return held.at[clip, slot, pl.ds(0, seq - 1)]

        def arrive(clip, slot):
            pltpu.make_async_copy(
                others(clip, slot), others(clip, slot), recv_sem.at[clip, slot]
            ).wait()
            pltpu.make_async_copy(
                held.at[clip, slot, me], held.at[clip, slot, me], own_sem.at[clip, slot]
            ).wait()

        def normalize(clip, slot, which):
            def step(i, carry):
                part = pl.ds(pl.multiple_of(i * 16, 16), 16)
                x = normed[slot - K, clip, part, :].astype(jnp.float32)
                dx = normed[slot + 1 - K, clip, part, :].astype(jnp.float32)
                gain = gains[which]
                inverse = lax.rsqrt(jnp.sum(x * x, axis=-1, keepdims=True) * (1.0 / width) + EPS)
                cross = jnp.sum(x * dx, axis=-1, keepdims=True) * (1.0 / width)
                normed[slot - K, clip, part, :] = (x * inverse * gain).astype(jnp.bfloat16)
                normed[slot + 1 - K, clip, part, :] = (
                    (dx * inverse - x * (inverse * inverse * inverse * cross)) * gain
                ).astype(jnp.bfloat16)
                return carry

            lax.fori_loop(0, rows // 16, step, 0)

        send(0, V)
        send(0, DV)

        pl.when(gate)(exchange_gains)

        @pl.when(jnp.logical_not(gate))
        def _():
            pltpu.make_async_copy(gathered, gathered, hand_recv).wait()

        for which in range(2):
            chunks = width // dp // DIM
            for owner in range(dp):
                for j in range(chunks):
                    at = (owner * chunks + j) * DIM
                    gains[which, :, at : at + DIM] = gathered[which, owner, j : j + 1, :]
        for copy in loads:
            copy.wait()

        normalize(0, K, 1)
        send(0, K)
        send(0, DK)
        normalize(0, Q, 0)
        send(0, Q)
        send(0, DQ)
        for clip in range(1, clips):
            normalize(clip, K, 1)
            normalize(clip, Q, 0)

        chip_row, half = me // plane, me % plane // 4

        def tile_of(i):
            crosses = i % 2
            row = lax.rem(chip_row + i // 2, tiles // 2)
            return row * 2 + (half + crosses) % 2

        def compute(clip, i):
            first = tile_of(i) * per_tile
            took = pl.ds(first, per_tile)

            def whole(slot):
                return held[clip, slot].reshape(seq * rows, DIM)

            out, dout = attend(
                held[clip, Q, took].reshape(TILE, DIM),
                held[clip, DQ, took].reshape(TILE, DIM),
                whole(K),
                whole(DK),
                whole(V),
                whole(DV),
            )
            results[clip, 0, took] = out.reshape(per_tile, rows, DIM)
            results[clip, 1, took] = dout.reshape(per_tile, rows, DIM)

        mine = pl.ds(pl.multiple_of(me * DIM, DIM), DIM)

        def give_back(clip, which, i):
            ref = (o_ref, do_ref)[which]
            first = tile_of(i) * per_tile
            for r in range(per_tile):
                token = first + r

                @pl.when(token != me)
                def _():
                    pltpu.make_async_remote_copy(
                        src_ref=results.at[clip, which, token],
                        dst_ref=ref.at[clip, :, mine],
                        send_sem=back_send.at[clip, which],
                        recv_sem=back_recv.at[clip, which],
                        device_id={"seq": token},
                        device_id_type=MESH,
                    ).start()

                @pl.when(token == me)
                def _():
                    pltpu.make_async_copy(
                        results.at[clip, which, token],
                        ref.at[clip, :, mine],
                        own_back.at[clip, which],
                    ).start()

        def loop(low, high, body):
            def step(i, carry):
                body(i)
                return carry

            lax.fori_loop(low, high, step, 0)

        send(1, V)
        arrive(0, V)
        send(1, DV)
        arrive(0, DV)
        send(1, K)
        arrive(0, K)
        arrive(0, DK)
        arrive(0, Q)
        arrive(0, DQ)
        send(1, DK)
        loop(0, 3, lambda i: compute(0, i))
        arrive(1, V)
        send(1, Q)
        loop(3, 6, lambda i: compute(0, i))
        arrive(1, DV)
        send(1, DQ)
        loop(6, tiles, lambda i: compute(0, i))
        arrive(1, K)
        arrive(1, DK)
        loop(0, tiles, lambda i: give_back(0, 0, i))
        arrive(1, Q)
        loop(0, tiles, lambda i: give_back(0, 1, i))
        arrive(1, DQ)

        def last(i):
            compute(1, i)
            give_back(1, 0, i)
            give_back(1, 1, i)

        loop(0, tiles, last)

        @pl.when(gate)
        def _():
            for which in range(2):
                other = gathered.at[which, pl.ds(0, dp - 1)]
                pltpu.make_async_copy(other, other, gain_send.at[which]).wait()

            def handed(r, carry):
                pltpu.make_async_copy(gathered, gathered, hand_send.at[r]).wait()
                return carry

            lax.fori_loop(1, seq // plane * 2, handed, 0)

        for clip in range(clips):
            for slot in range(6):
                pltpu.make_async_copy(
                    others(clip, slot), others(clip, slot), send_sem.at[clip, slot]
                ).wait()
            for which in range(2):
                own, some = results.at[clip, which, 0], results.at[clip, which, pl.ds(0, seq - 1)]
                pltpu.make_async_copy(some, some, back_send.at[clip, which]).wait()
                pltpu.make_async_copy(own, own, own_back.at[clip, which]).wait()
                pltpu.make_async_copy(some, some, back_recv.at[clip, which]).wait()

    return kernel


def solution(mesh):
    seq, dp = mesh.shape["seq"], mesh.shape["dp"]

    def on_device(q, k, v, dq, dk, dv, gq, gk):
        clips, rows, width = q.shape
        gq, gk = (gain.reshape(gain.shape[0] // DIM, DIM) for gain in (gq, gk))
        pieces = clips * seq * seq * rows
        rows_out = pl.pallas_call(
            make_kernel(seq, dp, clips, rows, width),
            out_shape=(pltpu.VMEM(q.shape, q.dtype),) * 2,
            in_specs=[pl.BlockSpec(memory_space=pl.ANY)] * 8,
            out_specs=(pl.BlockSpec(memory_space=pltpu.VMEM),) * 2,
            scratch_shapes=[
                pltpu.VMEM((4, clips, rows, width), jnp.bfloat16),
                pltpu.VMEM((2, dp) + gq.shape, jnp.float32),
                pltpu.VMEM((2, 1, width), jnp.float32),
                pltpu.VMEM((clips, 6, seq, rows, DIM), jnp.bfloat16),
                pltpu.VMEM((clips, 2, seq, rows, DIM), jnp.bfloat16),
                pltpu.SemaphoreType.DMA((6,)),
                pltpu.SemaphoreType.DMA((2,)),
                pltpu.SemaphoreType.DMA((2,)),
                pltpu.SemaphoreType.DMA((8,)),
                pltpu.SemaphoreType.DMA,
                pltpu.SemaphoreType.REGULAR,
                pltpu.SemaphoreType.DMA((clips, 6)),
                pltpu.SemaphoreType.DMA((clips, 6)),
                pltpu.SemaphoreType.DMA((clips, 2)),
                pltpu.SemaphoreType.DMA((clips, 2)),
                pltpu.SemaphoreType.DMA((clips, 6)),
                pltpu.SemaphoreType.DMA((clips, 2)),
            ],
            compiler_params=pltpu.CompilerParams(
                collective_id=0, has_side_effects=True, vmem_limit_bytes=48 * 2**20
            ),
            cost_estimate=pl.CostEstimate(
                flops=12 * pieces * seq * rows * DIM // seq,
                bytes_accessed=8 * 2 * clips * rows * width,
                transcendentals=pieces * seq * rows // seq,
            ),
        )(*(pltpu.with_memory_space_constraint(x, pltpu.HBM) for x in (q, k, v, dq, dk, dv, gq, gk)))
        out = jax.ShapeDtypeStruct(q.shape, q.dtype)
        return pl.pallas_call(
            write_out,
            out_shape=(out, out),
            in_specs=[pl.BlockSpec(memory_space=pltpu.VMEM)] * 2,
            out_specs=(pl.BlockSpec(memory_space=pl.ANY),) * 2,
            scratch_shapes=[pltpu.SemaphoreType.DMA((2,))],
        )(*(pltpu.with_memory_space_constraint(x, pltpu.VMEM) for x in rows_out))

    shard = P("dp", "seq", None)
    return jax.shard_map(
        on_device,
        mesh=mesh,
        in_specs=(shard,) * 6 + (P("dp"),) * 2,
        out_specs=(shard, shard),
        check_vma=False,
    )
```

```python
import jax
import jax.numpy as jnp
from jax import lax
from jax.experimental import pallas as pl
from jax.experimental.pallas import tpu as pltpu
from jax.sharding import PartitionSpec as P

EPS = 1e-06
DIM = 128
TILE = 256
MESH = pl.DeviceIdType.MESH
NT = (((1,), (1,)), ((), ()))
V, DV, K, DK, Q, DQ = range(6)


def attend(query, dquery, key, dkey, value, dvalue):
    scale = DIM**-0.5
    scores = lax.dot_general(query, key, NT, preferred_element_type=jnp.float32) * scale
    weights = jnp.exp(scores - jnp.max(scores, axis=-1, keepdims=True))
    weights = weights * (1.0 / jnp.sum(weights, axis=-1, keepdims=True))
    tangent = (
        lax.dot_general(
            jnp.concatenate([dquery, query], 1),
            jnp.concatenate([key, dkey], 1),
            NT,
            preferred_element_type=jnp.float32,
        )
        * scale
    )
    mean = jnp.sum(weights * tangent, axis=-1, keepdims=True)
    low = weights.astype(jnp.bfloat16)
    dlow = (weights * (tangent - mean)).astype(jnp.bfloat16)
    both = jnp.dot(low, jnp.concatenate([value, dvalue], 1), preferred_element_type=jnp.float32)
    dout = jnp.dot(dlow, value, preferred_element_type=jnp.float32) + both[:, DIM:]
    return both[:, :DIM].astype(jnp.bfloat16), dout.astype(jnp.bfloat16)


def write_out(a_ref, b_ref, o_ref, do_ref, sem):
    copies = [
        pltpu.make_async_copy(a_ref, o_ref, sem.at[0]),
        pltpu.make_async_copy(b_ref, do_ref, sem.at[1]),
    ]
    for copy in copies:
        copy.start()
    for copy in copies:
        copy.wait()


def make_kernel(seq, dp, clips, rows, width):
    per_tile = TILE // rows
    plane = 8
    tiles = seq // per_tile

    def kernel(
        q_ref,
        k_ref,
        v_ref,
        dq_ref,
        dk_ref,
        dv_ref,
        gq_ref,
        gk_ref,
        o_ref,
        do_ref,
        normed,
        gathered,
        gains,
        held,
        results,
        load_sem,
        gain_send,
        gain_recv,
        hand_send,
        hand_recv,
        entered,
        send_sem,
        recv_sem,
        back_send,
        back_recv,
        own_sem,
        own_back,
    ):
        me = lax.axis_index("seq")
        group = lax.axis_index("dp")
        gate = me % (plane + 2) == 0
        beside = me % (plane + 2) == 1
        barrier = pltpu.get_barrier_semaphore()

        def greet_seq(r, carry):
            peer = lax.rem(me - r + seq, seq)

            @pl.when(peer % (plane + 2) != 0)
            def _():
                pl.semaphore_signal(barrier, inc=1, device_id={"seq": peer}, device_id_type=MESH)

            return carry

        def greet_dp(r, carry):
            peer = lax.rem(group + r, dp)
            pl.semaphore_signal(barrier, inc=1, device_id={"dp": peer}, device_id_type=MESH)
            return carry

        lax.fori_loop(1, seq, greet_seq, 0)

        @pl.when(gate)
        def _():
            lax.fori_loop(1, dp, greet_dp, 0)

        sources = {K: k_ref, DK: dk_ref, Q: q_ref, DQ: dq_ref}
        loads = [
            pltpu.make_async_copy(ref, normed.at[slot - K], load_sem.at[slot - K])
            for slot, ref in sources.items()
        ]
        for copy in loads:
            copy.start()

        @pl.when(jnp.logical_not(gate))
        def _():
            pl.semaphore_wait(barrier, seq - 1)

        @pl.when(beside)
        def _():
            pl.semaphore_signal(entered, inc=1, device_id={"seq": me - 1}, device_id_type=MESH)

        @pl.when(gate)
        def _():
            pl.semaphore_wait(entered, 1)

        gain_loads = [
            pltpu.make_async_copy(ref, gathered.at[which, group], load_sem.at[4 + which])
            for which, ref in enumerate((gq_ref, gk_ref))
        ]

        def send_gains():
            for copy in gain_loads:
                copy.start()
            pl.semaphore_wait(barrier, dp - 1)
            for which, ref in enumerate((gq_ref, gk_ref)):

                def send_gain(r, carry):
                    peer = lax.rem(group + r, dp)
                    pltpu.make_async_remote_copy(
                        src_ref=ref,
                        dst_ref=gathered.at[which, group],
                        send_sem=gain_send.at[which],
                        recv_sem=gain_recv.at[which],
                        device_id={"dp": peer},
                        device_id_type=MESH,
                    ).start()
                    return carry

                lax.fori_loop(1, dp, send_gain, 0)

        def hand_gains():
            for which in range(2):
                gain_loads[which].wait()
                other = gathered.at[which, pl.ds(0, dp - 1)]
                pltpu.make_async_copy(other, other, gain_recv.at[which]).wait()

            def hand_on(r, carry):
                peer = lax.rem(me + lax.rem(r, 2) + r // 2 * plane, seq)
                pltpu.make_async_remote_copy(
                    src_ref=gathered,
                    dst_ref=gathered,
                    send_sem=hand_send.at[r],
                    recv_sem=hand_recv,
                    device_id={"seq": peer},
                    device_id_type=MESH,
                ).start()
                return carry

            lax.fori_loop(1, seq // plane * 2, hand_on, 0)

        def source(clip, slot, head):
            columns = pl.ds(pl.multiple_of(head * DIM, DIM), DIM)
            if slot == V:
                return v_ref.at[clip, :, columns]
            if slot == DV:
                return dv_ref.at[clip, :, columns]
            return normed.at[slot - K, clip, :, columns]

        def send(clip, slot):
            def one(r, carry):
                head = lax.rem(me + r, seq)
                pltpu.make_async_remote_copy(
                    src_ref=source(clip, slot, head),
                    dst_ref=held.at[clip, slot, me],
                    send_sem=send_sem.at[clip, slot],
                    recv_sem=recv_sem.at[clip, slot],
                    device_id={"seq": head},
                    device_id_type=MESH,
                ).start()
                return carry

            lax.fori_loop(1, seq, one, 0)
            pltpu.make_async_copy(
                source(clip, slot, me), held.at[clip, slot, me], own_sem.at[clip, slot]
            ).start()

        def others(clip, slot):
            return held.at[clip, slot, pl.ds(0, seq - 1)]

        def arrive(clip, slot):
            pltpu.make_async_copy(
                others(clip, slot), others(clip, slot), recv_sem.at[clip, slot]
            ).wait()
            pltpu.make_async_copy(
                held.at[clip, slot, me], held.at[clip, slot, me], own_sem.at[clip, slot]
            ).wait()

        def normalize(clip, slot, which):
            def step(i, carry):
                part = pl.ds(pl.multiple_of(i * 16, 16), 16)
                x = normed[slot - K, clip, part, :].astype(jnp.float32)
                dx = normed[slot + 1 - K, clip, part, :].astype(jnp.float32)
                gain = gains[which]
                inverse = lax.rsqrt(jnp.sum(x * x, axis=-1, keepdims=True) * (1.0 / width) + EPS)
                cross = jnp.sum(x * dx, axis=-1, keepdims=True) * (1.0 / width)
                normed[slot - K, clip, part, :] = (x * inverse * gain).astype(jnp.bfloat16)
                normed[slot + 1 - K, clip, part, :] = (
                    (dx * inverse - x * (inverse * inverse * inverse * cross)) * gain
                ).astype(jnp.bfloat16)
                return carry

            lax.fori_loop(0, rows // 16, step, 0)

        send(0, V)
        pl.when(gate)(send_gains)
        send(0, DV)
        pl.when(gate)(hand_gains)
        for clip in range(1, clips):
            send(clip, V)
            send(clip, DV)

        @pl.when(jnp.logical_not(gate))
        def _():
            pltpu.make_async_copy(gathered, gathered, hand_recv).wait()

        for which in range(2):
            chunks = width // dp // DIM
            for owner in range(dp):
                for j in range(chunks):
                    at = (owner * chunks + j) * DIM
                    gains[which, :, at : at + DIM] = gathered[which, owner, j : j + 1, :]
        for copy in loads:
            copy.wait()

        normalize(0, K, 1)
        send(0, K)
        send(0, DK)
        normalize(0, Q, 0)
        for clip in range(1, clips):
            normalize(clip, K, 1)
            normalize(clip, Q, 0)

        chip_row, half = me // plane, me % plane // 4

        def tile_of(i):
            crosses = i % 2
            row = lax.rem(chip_row + i // 2 + 1, tiles // 2)
            return row * 2 + (half + crosses) % 2

        def compute(clip, i):
            first = tile_of(i) * per_tile
            took = pl.ds(first, per_tile)

            def whole(slot):
                return held[clip, slot].reshape(seq * rows, DIM)

            out, dout = attend(
                held[clip, Q, took].reshape(TILE, DIM),
                held[clip, DQ, took].reshape(TILE, DIM),
                whole(K),
                whole(DK),
                whole(V),
                whole(DV),
            )
            results[clip, 0, took] = out.reshape(per_tile, rows, DIM)
            results[clip, 1, took] = dout.reshape(per_tile, rows, DIM)

        mine = pl.ds(pl.multiple_of(me * DIM, DIM), DIM)

        def give_back(clip, which, i):
            ref = (o_ref, do_ref)[which]
            first = tile_of(i) * per_tile
            for r in range(per_tile):
                token = first + half * r + (1 - half) * (per_tile - 1 - r)

                @pl.when(token != me)
                def _():
                    pltpu.make_async_remote_copy(
                        src_ref=results.at[clip, which, token],
                        dst_ref=ref.at[clip, :, mine],
                        send_sem=back_send.at[clip, which],
                        recv_sem=back_recv.at[clip, which],
                        device_id={"seq": token},
                        device_id_type=MESH,
                    ).start()

                @pl.when(token == me)
                def _():
                    pltpu.make_async_copy(
                        results.at[clip, which, token],
                        ref.at[clip, :, mine],
                        own_back.at[clip, which],
                    ).start()

        def loop(low, high, body):
            def step(i, carry):
                body(i)
                return carry

            lax.fori_loop(low, high, step, 0)

        arrive(0, V)
        send(0, Q)
        arrive(0, DV)
        send(0, DQ)
        arrive(1, V)
        send(1, K)
        arrive(1, DV)
        send(1, DK)
        arrive(0, K)
        send(1, Q)
        arrive(0, DK)
        send(1, DQ)
        arrive(0, Q)
        arrive(0, DQ)
        loop(0, tiles, lambda i: compute(0, i))
        arrive(1, K)
        arrive(1, DK)
        loop(0, tiles, lambda i: give_back(0, 0, i))
        arrive(1, Q)
        arrive(1, DQ)
        loop(0, tiles, lambda i: give_back(0, 1, i))

        def last(i):
            compute(1, i)
            give_back(1, 0, i)
            give_back(1, 1, i)

        loop(0, tiles, last)

        @pl.when(gate)
        def _():
            for which in range(2):
                other = gathered.at[which, pl.ds(0, dp - 1)]
                pltpu.make_async_copy(other, other, gain_send.at[which]).wait()

            def handed(r, carry):
                pltpu.make_async_copy(gathered, gathered, hand_send.at[r]).wait()
                return carry

            lax.fori_loop(1, seq // plane * 2, handed, 0)

        for clip in range(clips):
            for slot in range(6):
                pltpu.make_async_copy(
                    others(clip, slot), others(clip, slot), send_sem.at[clip, slot]
                ).wait()
            for which in range(2):
                own, some = results.at[clip, which, 0], results.at[clip, which, pl.ds(0, seq - 1)]
                pltpu.make_async_copy(some, some, back_send.at[clip, which]).wait()
                pltpu.make_async_copy(own, own, own_back.at[clip, which]).wait()
                pltpu.make_async_copy(some, some, back_recv.at[clip, which]).wait()

    return kernel


def solution(mesh):
    seq, dp = mesh.shape["seq"], mesh.shape["dp"]

    def on_device(q, k, v, dq, dk, dv, gq, gk):
        clips, rows, width = q.shape
        gq, gk = (gain.reshape(gain.shape[0] // DIM, DIM) for gain in (gq, gk))
        pieces = clips * seq * seq * rows
        rows_out = pl.pallas_call(
            make_kernel(seq, dp, clips, rows, width),
            out_shape=(pltpu.VMEM(q.shape, q.dtype),) * 2,
            in_specs=[pl.BlockSpec(memory_space=pl.ANY)] * 8,
            out_specs=(pl.BlockSpec(memory_space=pltpu.VMEM),) * 2,
            scratch_shapes=[
                pltpu.VMEM((4, clips, rows, width), jnp.bfloat16),
                pltpu.VMEM((2, dp) + gq.shape, jnp.float32),
                pltpu.VMEM((2, 1, width), jnp.float32),
                pltpu.VMEM((clips, 6, seq, rows, DIM), jnp.bfloat16),
                pltpu.VMEM((clips, 2, seq, rows, DIM), jnp.bfloat16),
                pltpu.SemaphoreType.DMA((6,)),
                pltpu.SemaphoreType.DMA((2,)),
                pltpu.SemaphoreType.DMA((2,)),
                pltpu.SemaphoreType.DMA((8,)),
                pltpu.SemaphoreType.DMA,
                pltpu.SemaphoreType.REGULAR,
                pltpu.SemaphoreType.DMA((clips, 6)),
                pltpu.SemaphoreType.DMA((clips, 6)),
                pltpu.SemaphoreType.DMA((clips, 2)),
                pltpu.SemaphoreType.DMA((clips, 2)),
                pltpu.SemaphoreType.DMA((clips, 6)),
                pltpu.SemaphoreType.DMA((clips, 2)),
            ],
            compiler_params=pltpu.CompilerParams(
                collective_id=0, has_side_effects=True, vmem_limit_bytes=48 * 2**20
            ),
            cost_estimate=pl.CostEstimate(
                flops=12 * pieces * seq * rows * DIM // seq,
                bytes_accessed=8 * 2 * clips * rows * width,
                transcendentals=pieces * seq * rows // seq,
            ),
        )(*(pltpu.with_memory_space_constraint(x, pltpu.HBM) for x in (q, k, v, dq, dk, dv, gq, gk)))
        out = jax.ShapeDtypeStruct(q.shape, q.dtype)
        return pl.pallas_call(
            write_out,
            out_shape=(out, out),
            in_specs=[pl.BlockSpec(memory_space=pltpu.VMEM)] * 2,
            out_specs=(pl.BlockSpec(memory_space=pl.ANY),) * 2,
            scratch_shapes=[pltpu.SemaphoreType.DMA((2,))],
        )(*(pltpu.with_memory_space_constraint(x, pltpu.VMEM) for x in rows_out))

    shard = P("dp", "seq", None)
    return jax.shard_map(
        on_device,
        mesh=mesh,
        in_specs=(shard,) * 6 + (P("dp"),) * 2,
        out_specs=(shard, shard),
        check_vma=False,
    )
```

```python
import jax
import jax.numpy as jnp
from jax import lax
from jax.experimental import pallas as pl
from jax.experimental.pallas import tpu as pltpu
from jax.sharding import PartitionSpec as P

EPS = 1e-06
DIM = 128
TILE = 256
MESH = pl.DeviceIdType.MESH
NT = (((1,), (1,)), ((), ()))
V, DV, K, DK, Q, DQ = range(6)


def attend(query, dquery, key, dkey, value, dvalue):
    scale = DIM**-0.5
    scores = lax.dot_general(query, key, NT, preferred_element_type=jnp.float32) * scale
    weights = jnp.exp(scores - jnp.max(scores, axis=-1, keepdims=True))
    weights = weights * (1.0 / jnp.sum(weights, axis=-1, keepdims=True))
    tangent = (
        lax.dot_general(
            jnp.concatenate([dquery, query], 1),
            jnp.concatenate([key, dkey], 1),
            NT,
            preferred_element_type=jnp.float32,
        )
        * scale
    )
    mean = jnp.sum(weights * tangent, axis=-1, keepdims=True)
    low = weights.astype(jnp.bfloat16)
    dlow = (weights * (tangent - mean)).astype(jnp.bfloat16)
    both = jnp.dot(low, jnp.concatenate([value, dvalue], 1), preferred_element_type=jnp.float32)
    dout = jnp.dot(dlow, value, preferred_element_type=jnp.float32) + both[:, DIM:]
    return both[:, :DIM].astype(jnp.bfloat16), dout.astype(jnp.bfloat16)


def write_out(a_ref, b_ref, o_ref, do_ref, sem):
    copies = [
        pltpu.make_async_copy(a_ref, o_ref, sem.at[0]),
        pltpu.make_async_copy(b_ref, do_ref, sem.at[1]),
    ]
    for copy in copies:
        copy.start()
    for copy in copies:
        copy.wait()


def make_kernel(seq, dp, clips, rows, width):
    per_tile = TILE // rows
    plane = 8
    tiles = seq // per_tile

    def kernel(
        q_ref,
        k_ref,
        v_ref,
        dq_ref,
        dk_ref,
        dv_ref,
        gq_ref,
        gk_ref,
        o_ref,
        do_ref,
        normed,
        gathered,
        gains,
        held,
        results,
        load_sem,
        gain_send,
        gain_recv,
        hand_send,
        hand_recv,
        entered,
        send_sem,
        recv_sem,
        back_send,
        back_recv,
        own_sem,
        own_back,
    ):
        me = lax.axis_index("seq")
        group = lax.axis_index("dp")
        row, z, core = me // plane, me % plane // 2, me % 2
        half = z // 2
        gate = me % (plane + 2) == 1
        listener = jnp.logical_and(core == 1, jnp.logical_not(gate))
        across = 2 - half
        barrier = pltpu.get_barrier_semaphore()

        def greet(peer):
            pl.semaphore_signal(barrier, inc=1, device_id={"seq": peer}, device_id_type=MESH)

        @pl.when(jnp.logical_or(z == 1, z == 2))
        def _():
            for k in range(2):
                greet(row * plane + (2 * (2 - z) + k) * 2)

        def greet_listener(r, carry):
            peer = lax.rem(me - r + seq, seq)
            pl.when(jnp.logical_and(peer % 2 == 1, peer % (plane + 2) != 1))(lambda: greet(peer))
            return carry

        def greet_dp(r, carry):
            peer = lax.rem(group + r, dp)
            pl.semaphore_signal(barrier, inc=1, device_id={"dp": peer}, device_id_type=MESH)
            return carry

        lax.fori_loop(1, seq, greet_listener, 0)

        @pl.when(gate)
        def _():
            lax.fori_loop(1, dp, greet_dp, 0)

        def source(clip, slot, head):
            columns = pl.ds(pl.multiple_of(head * DIM, DIM), DIM)
            if slot == V:
                return v_ref.at[clip, :, columns]
            if slot == DV:
                return dv_ref.at[clip, :, columns]
            return normed.at[slot - K, clip, :, columns]

        def send_one(clip, slot, head):
            pltpu.make_async_remote_copy(
                src_ref=source(clip, slot, head),
                dst_ref=held.at[clip, slot, me],
                send_sem=send_sem.at[clip, slot],
                recv_sem=recv_sem.at[clip, slot],
                device_id={"seq": head},
                device_id_type=MESH,
            ).start()

        def send_early():
            for clip in range(clips):
                for slot in (V, DV):
                    for k in range(2):
                        send_one(clip, slot, row * plane + across * 2 + k)

        @pl.when(core == 0)
        def _():
            pl.semaphore_wait(barrier, 2)
            send_early()

        sources = {K: k_ref, DK: dk_ref, Q: q_ref, DQ: dq_ref}
        loads = [
            pltpu.make_async_copy(ref, normed.at[slot - K], load_sem.at[slot - K])
            for slot, ref in sources.items()
        ]
        for copy in loads:
            copy.start()

        def admit(peer):
            pl.semaphore_signal(entered, inc=1, device_id={"seq": peer}, device_id_type=MESH)

        @pl.when(listener)
        def _():
            pl.semaphore_wait(barrier, seq - 1)
            admit(me - 1)

            @pl.when(row == lax.rem(z + 1, seq // plane))
            def _():
                admit(z * (plane + 2))
                admit(z * (plane + 2) + 1)

        @pl.when(jnp.logical_not(listener))
        def _():
            pl.semaphore_wait(entered, 1)

        gain_loads = [
            pltpu.make_async_copy(ref, gathered.at[which, group], load_sem.at[4 + which])
            for which, ref in enumerate((gq_ref, gk_ref))
        ]

        def send_gains():
            for copy in gain_loads:
                copy.start()
            pl.semaphore_wait(barrier, dp - 1)
            for which, ref in enumerate((gq_ref, gk_ref)):

                def send_gain(r, carry):
                    peer = lax.rem(group + r, dp)
                    pltpu.make_async_remote_copy(
                        src_ref=ref,
                        dst_ref=gathered.at[which, group],
                        send_sem=gain_send.at[which],
                        recv_sem=gain_recv.at[which],
                        device_id={"dp": peer},
                        device_id_type=MESH,
                    ).start()
                    return carry

                lax.fori_loop(1, dp, send_gain, 0)

        def hand_gains():
            for which in range(2):
                gain_loads[which].wait()
                other = gathered.at[which, pl.ds(0, dp - 1)]
                pltpu.make_async_copy(other, other, gain_recv.at[which]).wait()

            def hand_on(r, carry):
                step = lax.rem(r + 1, plane)
                peer = lax.rem(me - 1 + step % 2 + step // 2 * plane, seq)
                pltpu.make_async_remote_copy(
                    src_ref=gathered,
                    dst_ref=gathered,
                    send_sem=hand_send.at[r],
                    recv_sem=hand_recv,
                    device_id={"seq": peer},
                    device_id_type=MESH,
                ).start()
                return carry

            lax.fori_loop(1, seq // plane * 2, hand_on, 0)

        def send(clip, slot):
            def one(r, carry):
                head = lax.rem(me + r, seq)
                if slot in (V, DV):
                    sent = jnp.logical_and(core == 0, head // 2 == row * (plane // 2) + across)
                    pl.when(jnp.logical_not(sent))(lambda: send_one(clip, slot, head))
                else:
                    send_one(clip, slot, head)
                return carry

            lax.fori_loop(1, seq, one, 0)
            pltpu.make_async_copy(
                source(clip, slot, me), held.at[clip, slot, me], own_sem.at[clip, slot]
            ).start()

        def others(clip, slot):
            return held.at[clip, slot, pl.ds(0, seq - 1)]

        def arrive(clip, slot):
            pltpu.make_async_copy(
                others(clip, slot), others(clip, slot), recv_sem.at[clip, slot]
            ).wait()
            pltpu.make_async_copy(
                held.at[clip, slot, me], held.at[clip, slot, me], own_sem.at[clip, slot]
            ).wait()

        def normalize(clip, slot, which):
            def step(i, carry):
                part = pl.ds(pl.multiple_of(i * 16, 16), 16)
                x = normed[slot - K, clip, part, :].astype(jnp.float32)
                dx = normed[slot + 1 - K, clip, part, :].astype(jnp.float32)
                gain = gains[which]
                inverse = lax.rsqrt(jnp.sum(x * x, axis=-1, keepdims=True) * (1.0 / width) + EPS)
                cross = jnp.sum(x * dx, axis=-1, keepdims=True) * (1.0 / width)
                normed[slot - K, clip, part, :] = (x * inverse * gain).astype(jnp.bfloat16)
                normed[slot + 1 - K, clip, part, :] = (
                    (dx * inverse - x * (inverse * inverse * inverse * cross)) * gain
                ).astype(jnp.bfloat16)
                return carry

            lax.fori_loop(0, rows // 16, step, 0)

        send(0, V)
        pl.when(gate)(send_gains)
        send(0, DV)
        pl.when(gate)(hand_gains)
        for clip in range(1, clips):
            send(clip, V)
            send(clip, DV)

        @pl.when(jnp.logical_not(gate))
        def _():
            pltpu.make_async_copy(gathered, gathered, hand_recv).wait()

        for which in range(2):
            chunks = width // dp // DIM
            for owner in range(dp):
                for j in range(chunks):
                    at = (owner * chunks + j) * DIM
                    gains[which, :, at : at + DIM] = gathered[which, owner, j : j + 1, :]
        for copy in loads:
            copy.wait()

        normalize(0, K, 1)
        send(0, K)
        send(0, DK)
        normalize(0, Q, 0)
        for clip in range(1, clips):
            normalize(clip, K, 1)
            normalize(clip, Q, 0)

        def tile_of(i):
            crosses = i % 2
            return lax.rem(row + i // 2 + 1, tiles // 2) * 2 + (half + crosses) % 2

        def compute(clip, i):
            first = tile_of(i) * per_tile
            took = pl.ds(first, per_tile)

            def whole(slot):
                return held[clip, slot].reshape(seq * rows, DIM)

            out, dout = attend(
                held[clip, Q, took].reshape(TILE, DIM),
                held[clip, DQ, took].reshape(TILE, DIM),
                whole(K),
                whole(DK),
                whole(V),
                whole(DV),
            )
            results[clip, 0, took] = out.reshape(per_tile, rows, DIM)
            results[clip, 1, took] = dout.reshape(per_tile, rows, DIM)

        mine = pl.ds(pl.multiple_of(me * DIM, DIM), DIM)

        def give_back(clip, which, i):
            ref = (o_ref, do_ref)[which]
            first = tile_of(i) * per_tile
            for r in range(per_tile):
                token = first + half * r + (1 - half) * (per_tile - 1 - r)

                @pl.when(token != me)
                def _():
                    pltpu.make_async_remote_copy(
                        src_ref=results.at[clip, which, token],
                        dst_ref=ref.at[clip, :, mine],
                        send_sem=back_send.at[clip, which],
                        recv_sem=back_recv.at[clip, which],
                        device_id={"seq": token},
                        device_id_type=MESH,
                    ).start()

                @pl.when(token == me)
                def _():
                    pltpu.make_async_copy(
                        results.at[clip, which, token],
                        ref.at[clip, :, mine],
                        own_back.at[clip, which],
                    ).start()

        def loop(low, high, body):
            def step(i, carry):
                body(i)
                return carry

            lax.fori_loop(low, high, step, 0)

        arrive(0, V)
        send(0, Q)
        arrive(0, DV)
        send(0, DQ)
        arrive(1, V)
        send(1, K)
        arrive(1, DV)
        send(1, DK)
        arrive(0, K)
        send(1, Q)
        arrive(0, DK)
        send(1, DQ)
        arrive(0, Q)
        arrive(0, DQ)
        loop(0, tiles, lambda i: compute(0, i))
        arrive(1, K)
        arrive(1, DK)
        loop(0, tiles, lambda i: give_back(0, 0, i))
        arrive(1, Q)
        arrive(1, DQ)
        loop(0, tiles, lambda i: give_back(0, 1, i))

        def last(i):
            compute(1, i)
            give_back(1, 0, i)
            give_back(1, 1, i)

        loop(0, tiles, last)

        @pl.when(gate)
        def _():
            for which in range(2):
                other = gathered.at[which, pl.ds(0, dp - 1)]
                pltpu.make_async_copy(other, other, gain_send.at[which]).wait()

            def handed(r, carry):
                pltpu.make_async_copy(gathered, gathered, hand_send.at[r]).wait()
                return carry

            lax.fori_loop(1, seq // plane * 2, handed, 0)

        for clip in range(clips):
            for slot in range(6):
                pltpu.make_async_copy(
                    others(clip, slot), others(clip, slot), send_sem.at[clip, slot]
                ).wait()
            for which in range(2):
                own, some = results.at[clip, which, 0], results.at[clip, which, pl.ds(0, seq - 1)]
                pltpu.make_async_copy(some, some, back_send.at[clip, which]).wait()
                pltpu.make_async_copy(own, own, own_back.at[clip, which]).wait()
                pltpu.make_async_copy(some, some, back_recv.at[clip, which]).wait()

    return kernel


def solution(mesh):
    seq, dp = mesh.shape["seq"], mesh.shape["dp"]

    def on_device(q, k, v, dq, dk, dv, gq, gk):
        clips, rows, width = q.shape
        gq, gk = (gain.reshape(gain.shape[0] // DIM, DIM) for gain in (gq, gk))
        pieces = clips * seq * seq * rows
        rows_out = pl.pallas_call(
            make_kernel(seq, dp, clips, rows, width),
            out_shape=(pltpu.VMEM(q.shape, q.dtype),) * 2,
            in_specs=[pl.BlockSpec(memory_space=pl.ANY)] * 8,
            out_specs=(pl.BlockSpec(memory_space=pltpu.VMEM),) * 2,
            scratch_shapes=[
                pltpu.VMEM((4, clips, rows, width), jnp.bfloat16),
                pltpu.VMEM((2, dp) + gq.shape, jnp.float32),
                pltpu.VMEM((2, 1, width), jnp.float32),
                pltpu.VMEM((clips, 6, seq, rows, DIM), jnp.bfloat16),
                pltpu.VMEM((clips, 2, seq, rows, DIM), jnp.bfloat16),
                pltpu.SemaphoreType.DMA((6,)),
                pltpu.SemaphoreType.DMA((2,)),
                pltpu.SemaphoreType.DMA((2,)),
                pltpu.SemaphoreType.DMA((8,)),
                pltpu.SemaphoreType.DMA,
                pltpu.SemaphoreType.REGULAR,
                pltpu.SemaphoreType.DMA((clips, 6)),
                pltpu.SemaphoreType.DMA((clips, 6)),
                pltpu.SemaphoreType.DMA((clips, 2)),
                pltpu.SemaphoreType.DMA((clips, 2)),
                pltpu.SemaphoreType.DMA((clips, 6)),
                pltpu.SemaphoreType.DMA((clips, 2)),
            ],
            compiler_params=pltpu.CompilerParams(
                collective_id=0, has_side_effects=True, vmem_limit_bytes=48 * 2**20
            ),
            cost_estimate=pl.CostEstimate(
                flops=12 * pieces * seq * rows * DIM // seq,
                bytes_accessed=8 * 2 * clips * rows * width,
                transcendentals=pieces * seq * rows // seq,
            ),
        )(*(pltpu.with_memory_space_constraint(x, pltpu.HBM) for x in (q, k, v, dq, dk, dv, gq, gk)))
        out = jax.ShapeDtypeStruct(q.shape, q.dtype)
        return pl.pallas_call(
            write_out,
            out_shape=(out, out),
            in_specs=[pl.BlockSpec(memory_space=pltpu.VMEM)] * 2,
            out_specs=(pl.BlockSpec(memory_space=pl.ANY),) * 2,
            scratch_shapes=[pltpu.SemaphoreType.DMA((2,))],
        )(*(pltpu.with_memory_space_constraint(x, pltpu.VMEM) for x in rows_out))

    shard = P("dp", "seq", None)
    return jax.shard_map(
        on_device,
        mesh=mesh,
        in_specs=(shard,) * 6 + (P("dp"),) * 2,
        out_specs=(shard, shard),
        check_vma=False,
    )
```

```python
import jax
import jax.numpy as jnp
from jax import lax
from jax.experimental import pallas as pl
from jax.experimental.pallas import tpu as pltpu
from jax.sharding import PartitionSpec as P

EPS = 1e-06
DIM = 128
TILE = 256
MESH = pl.DeviceIdType.MESH
NT = (((1,), (1,)), ((), ()))
V, DV, K, DK, Q, DQ = range(6)


def attend(query, dquery, key, dkey, value, dvalue):
    scale = DIM**-0.5
    scores = lax.dot_general(query, key, NT, preferred_element_type=jnp.float32) * scale
    weights = jnp.exp(scores - jnp.max(scores, axis=-1, keepdims=True))
    weights = weights * (1.0 / jnp.sum(weights, axis=-1, keepdims=True))
    tangent = (
        lax.dot_general(
            jnp.concatenate([dquery, query], 1),
            jnp.concatenate([key, dkey], 1),
            NT,
            preferred_element_type=jnp.float32,
        )
        * scale
    )
    mean = jnp.sum(weights * tangent, axis=-1, keepdims=True)
    low = weights.astype(jnp.bfloat16)
    dlow = (weights * (tangent - mean)).astype(jnp.bfloat16)
    both = jnp.dot(low, jnp.concatenate([value, dvalue], 1), preferred_element_type=jnp.float32)
    dout = jnp.dot(dlow, value, preferred_element_type=jnp.float32) + both[:, DIM:]
    return both[:, :DIM].astype(jnp.bfloat16), dout.astype(jnp.bfloat16)


def write_out(a_ref, b_ref, o_ref, do_ref, sem):
    copies = [
        pltpu.make_async_copy(a_ref, o_ref, sem.at[0]),
        pltpu.make_async_copy(b_ref, do_ref, sem.at[1]),
    ]
    for copy in copies:
        copy.start()
    for copy in copies:
        copy.wait()


def make_kernel(seq, dp, clips, rows, width):
    per_tile = TILE // rows
    plane = 8
    tiles = seq // per_tile

    def kernel(
        q_ref,
        k_ref,
        v_ref,
        dq_ref,
        dk_ref,
        dv_ref,
        gq_ref,
        gk_ref,
        o_ref,
        do_ref,
        normed,
        gathered,
        gains,
        held,
        results,
        load_sem,
        gain_send,
        gain_recv,
        hand_send,
        hand_recv,
        entered,
        send_sem,
        recv_sem,
        back_send,
        back_recv,
        own_sem,
        own_back,
    ):
        me = lax.axis_index("seq")
        group = lax.axis_index("dp")
        row, z, core = me // plane, me % plane // 2, me % 2
        half = z // 2
        gate = me % (plane + 2) == 1
        listener = jnp.logical_and(core == 1, jnp.logical_not(gate))
        barrier = pltpu.get_barrier_semaphore()

        def greet(peer):
            pl.semaphore_signal(barrier, inc=1, device_id={"seq": peer}, device_id_type=MESH)

        @pl.when(z < 3)
        def _():
            for k in range(2):
                greet(row * plane + (2 * (1 - half) + k) * 2)

        def greet_listener(r, carry):
            peer = lax.rem(me - r + seq, seq)
            pl.when(jnp.logical_and(peer % 2 == 1, peer % (plane + 2) != 1))(lambda: greet(peer))
            return carry

        def greet_dp(r, carry):
            peer = lax.rem(group + r, dp)
            pl.semaphore_signal(barrier, inc=1, device_id={"dp": peer}, device_id_type=MESH)
            return carry

        lax.fori_loop(1, seq, greet_listener, 0)

        @pl.when(gate)
        def _():
            lax.fori_loop(1, dp, greet_dp, 0)

        def source(clip, slot, head):
            columns = pl.ds(pl.multiple_of(head * DIM, DIM), DIM)
            if slot == V:
                return v_ref.at[clip, :, columns]
            if slot == DV:
                return dv_ref.at[clip, :, columns]
            return normed.at[slot - K, clip, :, columns]

        def send_one(clip, slot, head):
            pltpu.make_async_remote_copy(
                src_ref=source(clip, slot, head),
                dst_ref=held.at[clip, slot, me],
                send_sem=send_sem.at[clip, slot],
                recv_sem=recv_sem.at[clip, slot],
                device_id={"seq": head},
                device_id_type=MESH,
            ).start()

        def send_early(to):
            for clip in range(clips):
                for slot in (V, DV):
                    for k in range(2):
                        send_one(clip, slot, row * plane + to * 2 + k)

        @pl.when(jnp.logical_and(core == 0, half == 0))
        def _():
            pl.semaphore_wait(barrier, 2)
            send_early(2)

        @pl.when(jnp.logical_and(core == 0, half == 1))
        def _():
            pl.semaphore_wait(barrier, 4)
            send_early(0)
            send_early(1)

        sources = {K: k_ref, DK: dk_ref, Q: q_ref, DQ: dq_ref}
        loads = [
            pltpu.make_async_copy(ref, normed.at[slot - K], load_sem.at[slot - K])
            for slot, ref in sources.items()
        ]
        for copy in loads:
            copy.start()

        def admit(peer):
            pl.semaphore_signal(entered, inc=1, device_id={"seq": peer}, device_id_type=MESH)

        @pl.when(listener)
        def _():
            pl.semaphore_wait(barrier, seq - 1)
            admit(me - 1)

            @pl.when(row == lax.rem(z + 1, seq // plane))
            def _():
                admit(z * (plane + 2))
                admit(z * (plane + 2) + 1)

        @pl.when(jnp.logical_not(listener))
        def _():
            pl.semaphore_wait(entered, 1)

        gain_loads = [
            pltpu.make_async_copy(ref, gathered.at[which, group], load_sem.at[4 + which])
            for which, ref in enumerate((gq_ref, gk_ref))
        ]

        def send_gains():
            for copy in gain_loads:
                copy.start()
            pl.semaphore_wait(barrier, dp - 1)
            for which, ref in enumerate((gq_ref, gk_ref)):

                def send_gain(r, carry):
                    peer = lax.rem(group + r, dp)
                    pltpu.make_async_remote_copy(
                        src_ref=ref,
                        dst_ref=gathered.at[which, group],
                        send_sem=gain_send.at[which],
                        recv_sem=gain_recv.at[which],
                        device_id={"dp": peer},
                        device_id_type=MESH,
                    ).start()
                    return carry

                lax.fori_loop(1, dp, send_gain, 0)

        def hand_gains():
            for which in range(2):
                gain_loads[which].wait()
                other = gathered.at[which, pl.ds(0, dp - 1)]
                pltpu.make_async_copy(other, other, gain_recv.at[which]).wait()

            def hand_on(r, carry):
                step = lax.rem(r + 1, plane)
                peer = lax.rem(me - 1 + step % 2 + step // 2 * plane, seq)
                pltpu.make_async_remote_copy(
                    src_ref=gathered,
                    dst_ref=gathered,
                    send_sem=hand_send.at[r],
                    recv_sem=hand_recv,
                    device_id={"seq": peer},
                    device_id_type=MESH,
                ).start()
                return carry

            lax.fori_loop(1, seq // plane * 2, hand_on, 0)

        def send(clip, slot):
            def one(r, carry):
                head = lax.rem(me + r, seq)
                if slot in (V, DV):
                    to = head % plane // 2
                    told = jnp.logical_or(to == 2 - 2 * half, to == 2 - half)
                    sent = jnp.logical_and(core == 0, jnp.logical_and(head // plane == row, told))
                    pl.when(jnp.logical_not(sent))(lambda: send_one(clip, slot, head))
                else:
                    send_one(clip, slot, head)
                return carry

            lax.fori_loop(1, seq, one, 0)
            pltpu.make_async_copy(
                source(clip, slot, me), held.at[clip, slot, me], own_sem.at[clip, slot]
            ).start()

        def others(clip, slot):
            return held.at[clip, slot, pl.ds(0, seq - 1)]

        def arrive(clip, slot):
            pltpu.make_async_copy(
                others(clip, slot), others(clip, slot), recv_sem.at[clip, slot]
            ).wait()
            pltpu.make_async_copy(
                held.at[clip, slot, me], held.at[clip, slot, me], own_sem.at[clip, slot]
            ).wait()

        def normalize(clip, slot, which):
            def step(i, carry):
                part = pl.ds(pl.multiple_of(i * 16, 16), 16)
                x = normed[slot - K, clip, part, :].astype(jnp.float32)
                dx = normed[slot + 1 - K, clip, part, :].astype(jnp.float32)
                gain = gains[which]
                inverse = lax.rsqrt(jnp.sum(x * x, axis=-1, keepdims=True) * (1.0 / width) + EPS)
                cross = jnp.sum(x * dx, axis=-1, keepdims=True) * (1.0 / width)
                normed[slot - K, clip, part, :] = (x * inverse * gain).astype(jnp.bfloat16)
                normed[slot + 1 - K, clip, part, :] = (
                    (dx * inverse - x * (inverse * inverse * inverse * cross)) * gain
                ).astype(jnp.bfloat16)
                return carry

            lax.fori_loop(0, rows // 16, step, 0)

        send(0, V)
        pl.when(gate)(send_gains)
        send(0, DV)
        pl.when(gate)(hand_gains)
        for clip in range(1, clips):
            send(clip, V)
            send(clip, DV)

        @pl.when(jnp.logical_not(gate))
        def _():
            pltpu.make_async_copy(gathered, gathered, hand_recv).wait()

        for which in range(2):
            chunks = width // dp // DIM
            for owner in range(dp):
                for j in range(chunks):
                    at = (owner * chunks + j) * DIM
                    gains[which, :, at : at + DIM] = gathered[which, owner, j : j + 1, :]
        for copy in loads:
            copy.wait()

        normalize(0, K, 1)
        send(0, K)
        send(0, DK)
        normalize(0, Q, 0)
        for clip in range(1, clips):
            normalize(clip, K, 1)
            normalize(clip, Q, 0)

        def tile_of(i):
            crosses = i % 2
            return lax.rem(row + i // 2 + 1, tiles // 2) * 2 + (half + crosses) % 2

        def compute(clip, i):
            first = tile_of(i) * per_tile
            took = pl.ds(first, per_tile)

            def whole(slot):
                return held[clip, slot].reshape(seq * rows, DIM)

            out, dout = attend(
                held[clip, Q, took].reshape(TILE, DIM),
                held[clip, DQ, took].reshape(TILE, DIM),
                whole(K),
                whole(DK),
                whole(V),
                whole(DV),
            )
            results[clip, 0, took] = out.reshape(per_tile, rows, DIM)
            results[clip, 1, took] = dout.reshape(per_tile, rows, DIM)

        mine = pl.ds(pl.multiple_of(me * DIM, DIM), DIM)

        def give_back(clip, which, i, pieces=range(per_tile)):
            ref = (o_ref, do_ref)[which]
            first = tile_of(i) * per_tile
            for r in pieces:
                token = first + half * r + (1 - half) * (per_tile - 1 - r)

                @pl.when(token != me)
                def _():
                    pltpu.make_async_remote_copy(
                        src_ref=results.at[clip, which, token],
                        dst_ref=ref.at[clip, :, mine],
                        send_sem=back_send.at[clip, which],
                        recv_sem=back_recv.at[clip, which],
                        device_id={"seq": token},
                        device_id_type=MESH,
                    ).start()

                @pl.when(token == me)
                def _():
                    pltpu.make_async_copy(
                        results.at[clip, which, token],
                        ref.at[clip, :, mine],
                        own_back.at[clip, which],
                    ).start()

        def loop(low, high, body):
            def step(i, carry):
                body(i)
                return carry

            lax.fori_loop(low, high, step, 0)

        arrive(0, V)
        send(0, Q)
        arrive(0, DV)
        send(0, DQ)
        arrive(1, V)
        send(1, K)
        arrive(1, DV)
        send(1, DK)
        arrive(0, K)
        send(1, Q)
        arrive(0, DK)
        send(1, DQ)
        arrive(0, Q)
        arrive(0, DQ)
        loop(0, tiles, lambda i: compute(0, i))
        arrive(1, K)
        arrive(1, DK)
        loop(0, tiles, lambda i: give_back(0, 0, i))
        arrive(1, Q)
        arrive(1, DQ)
        loop(0, tiles, lambda i: give_back(0, 1, i))

        def last(i):
            compute(1, i)
            for which in range(2):
                give_back(1, which, i, range(per_tile // 2))

            @pl.when(jnp.logical_or(half == 0, i % 2 == 0))
            def _():
                for which in range(2):
                    give_back(1, which, i, range(per_tile // 2, per_tile))

        loop(0, tiles, last)

        @pl.when(half == 1)
        def _():
            def rest(i):
                for which in range(2):
                    give_back(1, which, 2 * i + 1, range(per_tile // 2, per_tile))

            loop(0, tiles // 2, rest)

        @pl.when(gate)
        def _():
            for which in range(2):
                other = gathered.at[which, pl.ds(0, dp - 1)]
                pltpu.make_async_copy(other, other, gain_send.at[which]).wait()

            def handed(r, carry):
                pltpu.make_async_copy(gathered, gathered, hand_send.at[r]).wait()
                return carry

            lax.fori_loop(1, seq // plane * 2, handed, 0)

        for clip in range(clips):
            for slot in range(6):
                pltpu.make_async_copy(
                    others(clip, slot), others(clip, slot), send_sem.at[clip, slot]
                ).wait()
            for which in range(2):
                own, some = results.at[clip, which, 0], results.at[clip, which, pl.ds(0, seq - 1)]
                pltpu.make_async_copy(some, some, back_send.at[clip, which]).wait()
                pltpu.make_async_copy(own, own, own_back.at[clip, which]).wait()
                pltpu.make_async_copy(some, some, back_recv.at[clip, which]).wait()

    return kernel


def solution(mesh):
    seq, dp = mesh.shape["seq"], mesh.shape["dp"]

    def on_device(q, k, v, dq, dk, dv, gq, gk):
        clips, rows, width = q.shape
        gq, gk = (gain.reshape(gain.shape[0] // DIM, DIM) for gain in (gq, gk))
        pieces = clips * seq * seq * rows
        rows_out = pl.pallas_call(
            make_kernel(seq, dp, clips, rows, width),
            out_shape=(pltpu.VMEM(q.shape, q.dtype),) * 2,
            in_specs=[pl.BlockSpec(memory_space=pl.ANY)] * 8,
            out_specs=(pl.BlockSpec(memory_space=pltpu.VMEM),) * 2,
            scratch_shapes=[
                pltpu.VMEM((4, clips, rows, width), jnp.bfloat16),
                pltpu.VMEM((2, dp) + gq.shape, jnp.float32),
                pltpu.VMEM((2, 1, width), jnp.float32),
                pltpu.VMEM((clips, 6, seq, rows, DIM), jnp.bfloat16),
                pltpu.VMEM((clips, 2, seq, rows, DIM), jnp.bfloat16),
                pltpu.SemaphoreType.DMA((6,)),
                pltpu.SemaphoreType.DMA((2,)),
                pltpu.SemaphoreType.DMA((2,)),
                pltpu.SemaphoreType.DMA((8,)),
                pltpu.SemaphoreType.DMA,
                pltpu.SemaphoreType.REGULAR,
                pltpu.SemaphoreType.DMA((clips, 6)),
                pltpu.SemaphoreType.DMA((clips, 6)),
                pltpu.SemaphoreType.DMA((clips, 2)),
                pltpu.SemaphoreType.DMA((clips, 2)),
                pltpu.SemaphoreType.DMA((clips, 6)),
                pltpu.SemaphoreType.DMA((clips, 2)),
            ],
            compiler_params=pltpu.CompilerParams(
                collective_id=0, has_side_effects=True, vmem_limit_bytes=48 * 2**20
            ),
            cost_estimate=pl.CostEstimate(
                flops=12 * pieces * seq * rows * DIM // seq,
                bytes_accessed=8 * 2 * clips * rows * width,
                transcendentals=pieces * seq * rows // seq,
            ),
        )(*(pltpu.with_memory_space_constraint(x, pltpu.HBM) for x in (q, k, v, dq, dk, dv, gq, gk)))
        out = jax.ShapeDtypeStruct(q.shape, q.dtype)
        return pl.pallas_call(
            write_out,
            out_shape=(out, out),
            in_specs=[pl.BlockSpec(memory_space=pltpu.VMEM)] * 2,
            out_specs=(pl.BlockSpec(memory_space=pl.ANY),) * 2,
            scratch_shapes=[pltpu.SemaphoreType.DMA((2,))],
        )(*(pltpu.with_memory_space_constraint(x, pltpu.VMEM) for x in rows_out))

    shard = P("dp", "seq", None)
    return jax.shard_map(
        on_device,
        mesh=mesh,
        in_specs=(shard,) * 6 + (P("dp"),) * 2,
        out_specs=(shard, shard),
        check_vma=False,
    )
```

```python
import functools

import jax
import jax.numpy as jnp
from jax import lax
from jax.experimental import pallas as pl
from jax.experimental.pallas import tpu as pltpu
from jax.sharding import PartitionSpec as P

EPS = 1e-06
DIM = 128
TILE = 256
MESH = pl.DeviceIdType.MESH
NT = (((1,), (1,)), ((), ()))
V, DV, K, DK, Q, DQ = range(6)


def attend(query, dquery, key, dkey, value, dvalue):
    scale = DIM**-0.5
    scores = lax.dot_general(query, key, NT, preferred_element_type=jnp.float32) * scale
    weights = jnp.exp(scores - jnp.max(scores, axis=-1, keepdims=True))
    weights = weights * (1.0 / jnp.sum(weights, axis=-1, keepdims=True))
    tangent = (
        lax.dot_general(
            jnp.concatenate([dquery, query], 1),
            jnp.concatenate([key, dkey], 1),
            NT,
            preferred_element_type=jnp.float32,
        )
        * scale
    )
    mean = jnp.sum(weights * tangent, axis=-1, keepdims=True)
    low = weights.astype(jnp.bfloat16)
    dlow = (weights * (tangent - mean)).astype(jnp.bfloat16)
    both = jnp.dot(low, jnp.concatenate([value, dvalue], 1), preferred_element_type=jnp.float32)
    dout = jnp.dot(dlow, value, preferred_element_type=jnp.float32) + both[:, DIM:]
    return both[:, :DIM].astype(jnp.bfloat16), dout.astype(jnp.bfloat16)


def write_out(a_ref, b_ref, o_ref, do_ref, sem):
    copies = [
        pltpu.make_async_copy(a_ref, o_ref, sem.at[0]),
        pltpu.make_async_copy(b_ref, do_ref, sem.at[1]),
    ]
    for copy in copies:
        copy.start()
    for copy in copies:
        copy.wait()


def make_kernel(seq, dp, clips, rows, width):
    per_tile = TILE // rows
    plane = 8
    tiles = seq // per_tile

    def kernel(
        q_ref,
        k_ref,
        v_ref,
        dq_ref,
        dk_ref,
        dv_ref,
        gq_ref,
        gk_ref,
        o_ref,
        do_ref,
        normed,
        gathered,
        gains,
        held,
        results,
        load_sem,
        gain_send,
        gain_recv,
        hand_send,
        hand_recv,
        entered,
        send_sem,
        recv_sem,
        back_send,
        back_recv,
        own_sem,
        own_back,
    ):
        me = lax.axis_index("seq")
        group = lax.axis_index("dp")
        row, z = me // plane, me % plane // 2
        half = z // 2

        gates, listeners = ((at * plane + 3, at * plane + 5) for at in (2, 3))

        def is_gate(device):
            return jnp.logical_or(device == gates[0], device == gates[1])

        def is_listener(device):
            return jnp.logical_or(device == listeners[0], device == listeners[1])

        def is_common(device):
            return jnp.logical_not(jnp.logical_or(is_gate(device), is_listener(device)))

        def in_half(r):
            at = lax.rem(row * 4 + me % 4 + r, seq // 2)
            return at // 4 * plane + half * 4 + at % 4

        gate, listener, common = is_gate(me), is_listener(me), is_common(me)
        barrier = pltpu.get_barrier_semaphore()

        def greet(peer):
            pl.semaphore_signal(barrier, inc=1, device_id={"seq": peer}, device_id_type=MESH)

        for peer in listeners:
            pl.when(me != peer)(functools.partial(greet, peer))

        @pl.when(z < 3)
        def _():
            for k in range(4):
                peer = row * plane + (1 - half) * 4 + k
                pl.when(is_common(peer))(functools.partial(greet, peer))

        def greet_dp(r, carry):
            peer = lax.rem(group + r, dp)
            pl.semaphore_signal(barrier, inc=1, device_id={"dp": peer}, device_id_type=MESH)
            return carry

        @pl.when(gate)
        def _():
            lax.fori_loop(1, dp, greet_dp, 0)

        def source(clip, slot, head):
            columns = pl.ds(pl.multiple_of(head * DIM, DIM), DIM)
            if slot == V:
                return v_ref.at[clip, :, columns]
            if slot == DV:
                return dv_ref.at[clip, :, columns]
            return normed.at[slot - K, clip, :, columns]

        def send_one(clip, slot, head):
            pltpu.make_async_remote_copy(
                src_ref=source(clip, slot, head),
                dst_ref=held.at[clip, slot, me],
                send_sem=send_sem.at[clip, slot],
                recv_sem=recv_sem.at[clip, slot],
                device_id={"seq": head},
                device_id_type=MESH,
            ).start()

        def send_early(to):
            for clip in range(clips):
                for slot in (V, DV):
                    for k in range(2):
                        send_one(clip, slot, row * plane + to * 2 + k)

        @pl.when(jnp.logical_and(common, half == 0))
        def _():
            pl.semaphore_wait(barrier, 2)
            send_early(2)

        @pl.when(jnp.logical_and(common, half == 1))
        def _():
            pl.semaphore_wait(barrier, 4)
            send_early(0)
            send_early(1)

        sources = {K: k_ref, DK: dk_ref, Q: q_ref, DQ: dq_ref}
        loads = [
            pltpu.make_async_copy(ref, normed.at[slot - K], load_sem.at[slot - K])
            for slot, ref in sources.items()
        ]
        for copy in loads:
            copy.start()

        def admit(peer):
            pl.semaphore_signal(entered, inc=1, device_id={"seq": peer}, device_id_type=MESH)

        @pl.when(listener)
        def _():
            pl.semaphore_wait(barrier, seq - 1)

            def tell(r, carry):
                admit(in_half(r))
                return carry

            lax.fori_loop(1, seq // 2, tell, 0)

        @pl.when(jnp.logical_not(listener))
        def _():
            pl.semaphore_wait(entered, 1)

        gain_loads = [
            pltpu.make_async_copy(ref, gathered.at[which, group], load_sem.at[4 + which])
            for which, ref in enumerate((gq_ref, gk_ref))
        ]

        def send_gains():
            for copy in gain_loads:
                copy.start()
            pl.semaphore_wait(barrier, dp - 1)
            for which, ref in enumerate((gq_ref, gk_ref)):

                def send_gain(r, carry):
                    peer = lax.rem(group + r, dp)
                    pltpu.make_async_remote_copy(
                        src_ref=ref,
                        dst_ref=gathered.at[which, group],
                        send_sem=gain_send.at[which],
                        recv_sem=gain_recv.at[which],
                        device_id={"dp": peer},
                        device_id_type=MESH,
                    ).start()
                    return carry

                lax.fori_loop(1, dp, send_gain, 0)

        def hand_gains():
            for which in range(2):
                gain_loads[which].wait()
                other = gathered.at[which, pl.ds(0, dp - 1)]
                pltpu.make_async_copy(other, other, gain_recv.at[which]).wait()

            def hand_on(r, carry):
                pltpu.make_async_remote_copy(
                    src_ref=gathered,
                    dst_ref=gathered,
                    send_sem=hand_send.at[r],
                    recv_sem=hand_recv,
                    device_id={"seq": in_half(r)},
                    device_id_type=MESH,
                ).start()
                return carry

            lax.fori_loop(1, seq // 2, hand_on, 0)

        def send(clip, slot):
            def one(r, carry):
                head = lax.rem(me + r, seq)
                if slot in (V, DV):
                    to = head % plane // 2
                    told = jnp.logical_or(to == 2 - 2 * half, to == 2 - half)
                    sent = jnp.logical_and(common, jnp.logical_and(head // plane == row, told))
                    pl.when(jnp.logical_not(sent))(lambda: send_one(clip, slot, head))
                else:
                    send_one(clip, slot, head)
                return carry

            lax.fori_loop(1, seq, one, 0)
            pltpu.make_async_copy(
                source(clip, slot, me), held.at[clip, slot, me], own_sem.at[clip, slot]
            ).start()

        def others(clip, slot):
            return held.at[clip, slot, pl.ds(0, seq - 1)]

        def arrive(clip, slot):
            pltpu.make_async_copy(
                others(clip, slot), others(clip, slot), recv_sem.at[clip, slot]
            ).wait()
            pltpu.make_async_copy(
                held.at[clip, slot, me], held.at[clip, slot, me], own_sem.at[clip, slot]
            ).wait()

        def normalize(clip, slot, which):
            def step(i, carry):
                part = pl.ds(pl.multiple_of(i * 16, 16), 16)
                x = normed[slot - K, clip, part, :].astype(jnp.float32)
                dx = normed[slot + 1 - K, clip, part, :].astype(jnp.float32)
                gain = gains[which]
                inverse = lax.rsqrt(jnp.sum(x * x, axis=-1, keepdims=True) * (1.0 / width) + EPS)
                cross = jnp.sum(x * dx, axis=-1, keepdims=True) * (1.0 / width)
                normed[slot - K, clip, part, :] = (x * inverse * gain).astype(jnp.bfloat16)
                normed[slot + 1 - K, clip, part, :] = (
                    (dx * inverse - x * (inverse * inverse * inverse * cross)) * gain
                ).astype(jnp.bfloat16)
                return carry

            lax.fori_loop(0, rows // 16, step, 0)

        send(0, V)
        pl.when(gate)(send_gains)
        send(0, DV)
        pl.when(gate)(hand_gains)
        for clip in range(1, clips):
            send(clip, V)
            send(clip, DV)

        @pl.when(jnp.logical_not(gate))
        def _():
            pltpu.make_async_copy(gathered, gathered, hand_recv).wait()

        for which in range(2):
            chunks = width // dp // DIM
            for owner in range(dp):
                for j in range(chunks):
                    at = (owner * chunks + j) * DIM
                    gains[which, :, at : at + DIM] = gathered[which, owner, j : j + 1, :]
        for copy in loads:
            copy.wait()

        normalize(0, K, 1)
        send(0, K)
        send(0, DK)
        normalize(0, Q, 0)
        for clip in range(1, clips):
            normalize(clip, K, 1)
            normalize(clip, Q, 0)

        def tile_of(i):
            crosses, k = i % 2, i // 2
            outer = 1 - (row + 1) // 2 % 2
            served = k + (1 - outer) * (1 - 2 * (k % 2))
            near = lax.rem(row + k + 1, tiles // 2)
            return (crosses * served + (1 - crosses) * near) * 2 + (half + crosses) % 2

        def compute(clip, i):
            first = tile_of(i) * per_tile
            took = pl.ds(first, per_tile)

            def whole(slot):
                return held[clip, slot].reshape(seq * rows, DIM)

            out, dout = attend(
                held[clip, Q, took].reshape(TILE, DIM),
                held[clip, DQ, took].reshape(TILE, DIM),
                whole(K),
                whole(DK),
                whole(V),
                whole(DV),
            )
            results[clip, 0, took] = out.reshape(per_tile, rows, DIM)
            results[clip, 1, took] = dout.reshape(per_tile, rows, DIM)

        mine = pl.ds(pl.multiple_of(me * DIM, DIM), DIM)

        def give_back(clip, which, i, pieces=range(per_tile)):
            ref = (o_ref, do_ref)[which]
            first = tile_of(i) * per_tile
            for r in pieces:
                token = first + half * r + (1 - half) * (per_tile - 1 - r)

                @pl.when(token != me)
                def _():
                    pltpu.make_async_remote_copy(
                        src_ref=results.at[clip, which, token],
                        dst_ref=ref.at[clip, :, mine],
                        send_sem=back_send.at[clip, which],
                        recv_sem=back_recv.at[clip, which],
                        device_id={"seq": token},
                        device_id_type=MESH,
                    ).start()

                @pl.when(token == me)
                def _():
                    pltpu.make_async_copy(
                        results.at[clip, which, token],
                        ref.at[clip, :, mine],
                        own_back.at[clip, which],
                    ).start()

        def loop(low, high, body):
            def step(i, carry):
                body(i)
                return carry

            lax.fori_loop(low, high, step, 0)

        arrive(0, V)
        send(0, Q)
        arrive(0, DV)
        send(0, DQ)
        arrive(1, V)
        send(1, K)
        arrive(1, DV)
        send(1, DK)
        arrive(0, K)
        send(1, Q)
        arrive(0, DK)
        send(1, DQ)
        arrive(0, Q)
        arrive(0, DQ)
        loop(0, tiles, lambda i: compute(0, i))
        arrive(1, K)
        arrive(1, DK)
        loop(0, tiles, lambda i: give_back(0, 0, i))
        arrive(1, Q)
        arrive(1, DQ)
        loop(0, tiles, lambda i: give_back(0, 1, i))

        def last(i):
            compute(1, i)
            for which in range(2):
                give_back(1, which, i, range(per_tile // 2))

            @pl.when(jnp.logical_or(half == 0, i % 2 == 0))
            def _():
                for which in range(2):
                    give_back(1, which, i, range(per_tile // 2, per_tile))

        loop(0, tiles, last)

        @pl.when(half == 1)
        def _():
            def rest(i):
                for which in range(2):
                    give_back(1, which, 2 * i + 1, range(per_tile // 2, per_tile))

            loop(0, tiles // 2, rest)

        @pl.when(gate)
        def _():
            for which in range(2):
                other = gathered.at[which, pl.ds(0, dp - 1)]
                pltpu.make_async_copy(other, other, gain_send.at[which]).wait()

            def handed(r, carry):
                pltpu.make_async_copy(gathered, gathered, hand_send.at[r]).wait()
                return carry

            lax.fori_loop(1, seq // 2, handed, 0)

        for clip in range(clips):
            for slot in range(6):
                pltpu.make_async_copy(
                    others(clip, slot), others(clip, slot), send_sem.at[clip, slot]
                ).wait()
            for which in range(2):
                own, some = results.at[clip, which, 0], results.at[clip, which, pl.ds(0, seq - 1)]
                pltpu.make_async_copy(some, some, back_send.at[clip, which]).wait()
                pltpu.make_async_copy(own, own, own_back.at[clip, which]).wait()
                pltpu.make_async_copy(some, some, back_recv.at[clip, which]).wait()

    return kernel


def solution(mesh):
    seq, dp = mesh.shape["seq"], mesh.shape["dp"]

    def on_device(q, k, v, dq, dk, dv, gq, gk):
        clips, rows, width = q.shape
        gq, gk = (gain.reshape(gain.shape[0] // DIM, DIM) for gain in (gq, gk))
        pieces = clips * seq * seq * rows
        rows_out = pl.pallas_call(
            make_kernel(seq, dp, clips, rows, width),
            out_shape=(pltpu.VMEM(q.shape, q.dtype),) * 2,
            in_specs=[pl.BlockSpec(memory_space=pl.ANY)] * 8,
            out_specs=(pl.BlockSpec(memory_space=pltpu.VMEM),) * 2,
            scratch_shapes=[
                pltpu.VMEM((4, clips, rows, width), jnp.bfloat16),
                pltpu.VMEM((2, dp) + gq.shape, jnp.float32),
                pltpu.VMEM((2, 1, width), jnp.float32),
                pltpu.VMEM((clips, 6, seq, rows, DIM), jnp.bfloat16),
                pltpu.VMEM((clips, 2, seq, rows, DIM), jnp.bfloat16),
                pltpu.SemaphoreType.DMA((6,)),
                pltpu.SemaphoreType.DMA((2,)),
                pltpu.SemaphoreType.DMA((2,)),
                pltpu.SemaphoreType.DMA((seq // 2,)),
                pltpu.SemaphoreType.DMA,
                pltpu.SemaphoreType.REGULAR,
                pltpu.SemaphoreType.DMA((clips, 6)),
                pltpu.SemaphoreType.DMA((clips, 6)),
                pltpu.SemaphoreType.DMA((clips, 2)),
                pltpu.SemaphoreType.DMA((clips, 2)),
                pltpu.SemaphoreType.DMA((clips, 6)),
                pltpu.SemaphoreType.DMA((clips, 2)),
            ],
            compiler_params=pltpu.CompilerParams(
                collective_id=0, has_side_effects=True, vmem_limit_bytes=48 * 2**20
            ),
            cost_estimate=pl.CostEstimate(
                flops=12 * pieces * seq * rows * DIM // seq,
                bytes_accessed=8 * 2 * clips * rows * width,
                transcendentals=pieces * seq * rows // seq,
            ),
        )(*(pltpu.with_memory_space_constraint(x, pltpu.HBM) for x in (q, k, v, dq, dk, dv, gq, gk)))
        out = jax.ShapeDtypeStruct(q.shape, q.dtype)
        return pl.pallas_call(
            write_out,
            out_shape=(out, out),
            in_specs=[pl.BlockSpec(memory_space=pltpu.VMEM)] * 2,
            out_specs=(pl.BlockSpec(memory_space=pl.ANY),) * 2,
            scratch_shapes=[pltpu.SemaphoreType.DMA((2,))],
        )(*(pltpu.with_memory_space_constraint(x, pltpu.VMEM) for x in rows_out))

    shard = P("dp", "seq", None)
    return jax.shard_map(
        on_device,
        mesh=mesh,
        in_specs=(shard,) * 6 + (P("dp"),) * 2,
        out_specs=(shard, shard),
        check_vma=False,
    )
```

```python
import functools

import jax
import jax.numpy as jnp
from jax import lax
from jax.experimental import pallas as pl
from jax.experimental.pallas import tpu as pltpu
from jax.sharding import PartitionSpec as P

EPS = 1e-06
DIM = 128
TILE = 256
MESH = pl.DeviceIdType.MESH
NT = (((1,), (1,)), ((), ()))
V, DV, K, DK, Q, DQ = range(6)


def attend(query, dquery, key, dkey, value, dvalue):
    scale = DIM**-0.5
    scores = lax.dot_general(query, key, NT, preferred_element_type=jnp.float32) * scale
    weights = jnp.exp(scores - jnp.max(scores, axis=-1, keepdims=True))
    weights = weights * (1.0 / jnp.sum(weights, axis=-1, keepdims=True))
    tangent = (
        lax.dot_general(
            jnp.concatenate([dquery, query], 1),
            jnp.concatenate([key, dkey], 1),
            NT,
            preferred_element_type=jnp.float32,
        )
        * scale
    )
    mean = jnp.sum(weights * tangent, axis=-1, keepdims=True)
    low = weights.astype(jnp.bfloat16)
    dlow = (weights * (tangent - mean)).astype(jnp.bfloat16)
    both = jnp.dot(low, jnp.concatenate([value, dvalue], 1), preferred_element_type=jnp.float32)
    dout = jnp.dot(dlow, value, preferred_element_type=jnp.float32) + both[:, DIM:]
    return both[:, :DIM].astype(jnp.bfloat16), dout.astype(jnp.bfloat16)


def write_out(a_ref, b_ref, o_ref, do_ref, sem):
    copies = [
        pltpu.make_async_copy(a_ref, o_ref, sem.at[0]),
        pltpu.make_async_copy(b_ref, do_ref, sem.at[1]),
    ]
    for copy in copies:
        copy.start()
    for copy in copies:
        copy.wait()


def make_kernel(seq, dp, clips, rows, width):
    per_tile = TILE // rows
    plane = 8
    tiles = seq // per_tile

    def kernel(
        q_ref,
        k_ref,
        v_ref,
        dq_ref,
        dk_ref,
        dv_ref,
        gq_ref,
        gk_ref,
        o_ref,
        do_ref,
        normed,
        gathered,
        gains,
        held,
        results,
        load_sem,
        gain_send,
        gain_recv,
        hand_send,
        hand_recv,
        entered,
        send_sem,
        recv_sem,
        back_send,
        back_recv,
        own_sem,
        own_back,
    ):
        me = lax.axis_index("seq")
        group = lax.axis_index("dp")
        row, z = me // plane, me % plane // 2
        half = z // 2

        gates, listeners = ((at * plane + 3, at * plane + 5) for at in (2, 3))

        def is_gate(device):
            return jnp.logical_or(device == gates[0], device == gates[1])

        def is_listener(device):
            return jnp.logical_or(device == listeners[0], device == listeners[1])

        def is_common(device):
            return jnp.logical_not(jnp.logical_or(is_gate(device), is_listener(device)))

        def in_half(r):
            at = lax.rem(row * 4 + me % 4 + r, seq // 2)
            return at // 4 * plane + half * 4 + at % 4

        gate, listener, common = is_gate(me), is_listener(me), is_common(me)
        barrier = pltpu.get_barrier_semaphore()

        def greet(peer):
            pl.semaphore_signal(barrier, inc=1, device_id={"seq": peer}, device_id_type=MESH)

        for peer in listeners:
            pl.when(me != peer)(functools.partial(greet, peer))

        @pl.when(z < 3)
        def _():
            for k in range(4):
                peer = row * plane + (1 - half) * 4 + k
                pl.when(is_common(peer))(functools.partial(greet, peer))

        def greet_dp(r, carry):
            peer = lax.rem(group + r, dp)
            pl.semaphore_signal(barrier, inc=1, device_id={"dp": peer}, device_id_type=MESH)
            return carry

        @pl.when(gate)
        def _():
            lax.fori_loop(1, dp, greet_dp, 0)

        def source(clip, slot, head):
            columns = pl.ds(pl.multiple_of(head * DIM, DIM), DIM)
            if slot == V:
                return v_ref.at[clip, :, columns]
            if slot == DV:
                return dv_ref.at[clip, :, columns]
            return normed.at[slot - K, clip, :, columns]

        def send_one(clip, slot, head):
            pltpu.make_async_remote_copy(
                src_ref=source(clip, slot, head),
                dst_ref=held.at[clip, slot, me],
                send_sem=send_sem.at[clip, slot],
                recv_sem=recv_sem.at[clip, slot],
                device_id={"seq": head},
                device_id_type=MESH,
            ).start()

        def send_early(to):
            for clip in range(clips):
                for slot in (V, DV):
                    for k in range(2):
                        send_one(clip, slot, row * plane + to * 2 + k)

        @pl.when(jnp.logical_and(common, half == 0))
        def _():
            pl.semaphore_wait(barrier, 2)
            send_early(2)

        @pl.when(jnp.logical_and(common, half == 1))
        def _():
            pl.semaphore_wait(barrier, 4)
            send_early(0)
            send_early(1)

        sources = {K: k_ref, DK: dk_ref, Q: q_ref, DQ: dq_ref}
        loads = [
            pltpu.make_async_copy(ref, normed.at[slot - K], load_sem.at[slot - K])
            for slot, ref in sources.items()
        ]
        for copy in loads:
            copy.start()

        def admit(peer):
            pl.semaphore_signal(entered, inc=1, device_id={"seq": peer}, device_id_type=MESH)

        @pl.when(listener)
        def _():
            pl.semaphore_wait(barrier, seq - 1)

            def tell(r, carry):
                admit(in_half(r))
                return carry

            lax.fori_loop(1, seq // 2, tell, 0)

        @pl.when(jnp.logical_not(listener))
        def _():
            pl.semaphore_wait(entered, 1)

        gain_loads = [
            pltpu.make_async_copy(ref, gathered.at[which, group], load_sem.at[4 + which])
            for which, ref in enumerate((gq_ref, gk_ref))
        ]

        def send_gains():
            for copy in gain_loads:
                copy.start()
            pl.semaphore_wait(barrier, dp - 1)
            for which, ref in enumerate((gq_ref, gk_ref)):

                def send_gain(r, carry):
                    peer = lax.rem(group + r, dp)
                    pltpu.make_async_remote_copy(
                        src_ref=ref,
                        dst_ref=gathered.at[which, group],
                        send_sem=gain_send.at[which],
                        recv_sem=gain_recv.at[which],
                        device_id={"dp": peer},
                        device_id_type=MESH,
                    ).start()
                    return carry

                lax.fori_loop(1, dp, send_gain, 0)

        def hand_gains():
            for which in range(2):
                gain_loads[which].wait()
                other = gathered.at[which, pl.ds(0, dp - 1)]
                pltpu.make_async_copy(other, other, gain_recv.at[which]).wait()

            def hand_on(r, carry):
                pltpu.make_async_remote_copy(
                    src_ref=gathered,
                    dst_ref=gathered,
                    send_sem=hand_send.at[r],
                    recv_sem=hand_recv,
                    device_id={"seq": in_half(r)},
                    device_id_type=MESH,
                ).start()
                return carry

            lax.fori_loop(1, seq // 2, hand_on, 0)

        def send(clip, slot):
            def one(r, carry):
                head = lax.rem(me + r, seq)
                if slot in (V, DV):
                    to = head % plane // 2
                    told = jnp.logical_or(to == 2 - 2 * half, to == 2 - half)
                    sent = jnp.logical_and(common, jnp.logical_and(head // plane == row, told))
                    pl.when(jnp.logical_not(sent))(lambda: send_one(clip, slot, head))
                else:
                    send_one(clip, slot, head)
                return carry

            lax.fori_loop(1, seq, one, 0)
            pltpu.make_async_copy(
                source(clip, slot, me), held.at[clip, slot, me], own_sem.at[clip, slot]
            ).start()

        def others(clip, slot):
            return held.at[clip, slot, pl.ds(0, seq - 1)]

        def arrive(clip, slot):
            pltpu.make_async_copy(
                others(clip, slot), others(clip, slot), recv_sem.at[clip, slot]
            ).wait()
            pltpu.make_async_copy(
                held.at[clip, slot, me], held.at[clip, slot, me], own_sem.at[clip, slot]
            ).wait()

        def normalize(clip, slot, which):
            def step(i, carry):
                part = pl.ds(pl.multiple_of(i * 16, 16), 16)
                x = normed[slot - K, clip, part, :].astype(jnp.float32)
                dx = normed[slot + 1 - K, clip, part, :].astype(jnp.float32)
                gain = gains[which]
                inverse = lax.rsqrt(jnp.sum(x * x, axis=-1, keepdims=True) * (1.0 / width) + EPS)
                cross = jnp.sum(x * dx, axis=-1, keepdims=True) * (1.0 / width)
                normed[slot - K, clip, part, :] = (x * inverse * gain).astype(jnp.bfloat16)
                normed[slot + 1 - K, clip, part, :] = (
                    (dx * inverse - x * (inverse * inverse * inverse * cross)) * gain
                ).astype(jnp.bfloat16)
                return carry

            lax.fori_loop(0, rows // 16, step, 0)

        send(0, V)
        pl.when(gate)(send_gains)
        send(0, DV)
        pl.when(gate)(hand_gains)
        for clip in range(1, clips):
            send(clip, V)
            send(clip, DV)

        @pl.when(jnp.logical_not(gate))
        def _():
            pltpu.make_async_copy(gathered, gathered, hand_recv).wait()

        for which in range(2):
            chunks = width // dp // DIM
            for owner in range(dp):
                for j in range(chunks):
                    at = (owner * chunks + j) * DIM
                    gains[which, :, at : at + DIM] = gathered[which, owner, j : j + 1, :]
        for copy in loads:
            copy.wait()

        normalize(0, K, 1)
        send(0, K)
        send(0, DK)
        normalize(0, Q, 0)
        for clip in range(1, clips):
            normalize(clip, K, 1)
            normalize(clip, Q, 0)

        def tile_of(i):
            crosses, k = i % 2, i // 2
            outer = 1 - (row + 1) // 2 % 2
            near = lax.rem(row + k + 1, tiles // 2)
            served = outer * k + (1 - outer) * near
            return (crosses * served + (1 - crosses) * near) * 2 + (half + crosses) % 2

        def compute(clip, i):
            first = tile_of(i) * per_tile
            took = pl.ds(first, per_tile)

            def whole(slot):
                return held[clip, slot].reshape(seq * rows, DIM)

            out, dout = attend(
                held[clip, Q, took].reshape(TILE, DIM),
                held[clip, DQ, took].reshape(TILE, DIM),
                whole(K),
                whole(DK),
                whole(V),
                whole(DV),
            )
            results[clip, 0, took] = out.reshape(per_tile, rows, DIM)
            results[clip, 1, took] = dout.reshape(per_tile, rows, DIM)

        mine = pl.ds(pl.multiple_of(me * DIM, DIM), DIM)

        def give_back(clip, which, i, pieces=range(per_tile)):
            ref = (o_ref, do_ref)[which]
            first = tile_of(i) * per_tile
            for r in pieces:
                token = first + half * r + (1 - half) * (per_tile - 1 - r)

                @pl.when(token != me)
                def _():
                    pltpu.make_async_remote_copy(
                        src_ref=results.at[clip, which, token],
                        dst_ref=ref.at[clip, :, mine],
                        send_sem=back_send.at[clip, which],
                        recv_sem=back_recv.at[clip, which],
                        device_id={"seq": token},
                        device_id_type=MESH,
                    ).start()

                @pl.when(token == me)
                def _():
                    pltpu.make_async_copy(
                        results.at[clip, which, token],
                        ref.at[clip, :, mine],
                        own_back.at[clip, which],
                    ).start()

        def loop(low, high, body):
            def step(i, carry):
                body(i)
                return carry

            lax.fori_loop(low, high, step, 0)

        arrive(0, V)
        send(0, Q)
        arrive(0, DV)
        send(0, DQ)
        arrive(1, V)
        send(1, K)
        arrive(1, DV)
        send(1, DK)
        arrive(0, K)
        send(1, Q)
        arrive(0, DK)
        send(1, DQ)
        arrive(0, Q)
        arrive(0, DQ)
        loop(0, tiles, lambda i: compute(0, i))
        arrive(1, K)
        arrive(1, DK)
        loop(0, tiles, lambda i: give_back(0, 0, i))
        arrive(1, Q)
        arrive(1, DQ)
        loop(0, tiles, lambda i: give_back(0, 1, i))

        inner = jnp.logical_or(z == 1, z == 2)

        def last(i):
            compute(1, i)
            for which in range(2):
                give_back(1, which, i, range(per_tile // 2))

            @pl.when(jnp.logical_or(inner, i % 2 == 0))
            def _():
                for which in range(2):
                    give_back(1, which, i, range(per_tile // 2, per_tile))

        loop(0, tiles, last)

        @pl.when(jnp.logical_not(inner))
        def _():
            def rest(i):
                for which in range(2):
                    give_back(1, which, 2 * i + 1, range(per_tile // 2, per_tile))

            loop(0, tiles // 2, rest)

        @pl.when(gate)
        def _():
            for which in range(2):
                other = gathered.at[which, pl.ds(0, dp - 1)]
                pltpu.make_async_copy(other, other, gain_send.at[which]).wait()

            def handed(r, carry):
                pltpu.make_async_copy(gathered, gathered, hand_send.at[r]).wait()
                return carry

            lax.fori_loop(1, seq // 2, handed, 0)

        for clip in range(clips):
            for slot in range(6):
                pltpu.make_async_copy(
                    others(clip, slot), others(clip, slot), send_sem.at[clip, slot]
                ).wait()
            for which in range(2):
                own, some = results.at[clip, which, 0], results.at[clip, which, pl.ds(0, seq - 1)]
                pltpu.make_async_copy(some, some, back_send.at[clip, which]).wait()
                pltpu.make_async_copy(own, own, own_back.at[clip, which]).wait()
                pltpu.make_async_copy(some, some, back_recv.at[clip, which]).wait()

    return kernel


def solution(mesh):
    seq, dp = mesh.shape["seq"], mesh.shape["dp"]

    def on_device(q, k, v, dq, dk, dv, gq, gk):
        clips, rows, width = q.shape
        gq, gk = (gain.reshape(gain.shape[0] // DIM, DIM) for gain in (gq, gk))
        pieces = clips * seq * seq * rows
        rows_out = pl.pallas_call(
            make_kernel(seq, dp, clips, rows, width),
            out_shape=(pltpu.VMEM(q.shape, q.dtype),) * 2,
            in_specs=[pl.BlockSpec(memory_space=pl.ANY)] * 8,
            out_specs=(pl.BlockSpec(memory_space=pltpu.VMEM),) * 2,
            scratch_shapes=[
                pltpu.VMEM((4, clips, rows, width), jnp.bfloat16),
                pltpu.VMEM((2, dp) + gq.shape, jnp.float32),
                pltpu.VMEM((2, 1, width), jnp.float32),
                pltpu.VMEM((clips, 6, seq, rows, DIM), jnp.bfloat16),
                pltpu.VMEM((clips, 2, seq, rows, DIM), jnp.bfloat16),
                pltpu.SemaphoreType.DMA((6,)),
                pltpu.SemaphoreType.DMA((2,)),
                pltpu.SemaphoreType.DMA((2,)),
                pltpu.SemaphoreType.DMA((seq // 2,)),
                pltpu.SemaphoreType.DMA,
                pltpu.SemaphoreType.REGULAR,
                pltpu.SemaphoreType.DMA((clips, 6)),
                pltpu.SemaphoreType.DMA((clips, 6)),
                pltpu.SemaphoreType.DMA((clips, 2)),
                pltpu.SemaphoreType.DMA((clips, 2)),
                pltpu.SemaphoreType.DMA((clips, 6)),
                pltpu.SemaphoreType.DMA((clips, 2)),
            ],
            compiler_params=pltpu.CompilerParams(
                collective_id=0, has_side_effects=True, vmem_limit_bytes=48 * 2**20
            ),
            cost_estimate=pl.CostEstimate(
                flops=12 * pieces * seq * rows * DIM // seq,
                bytes_accessed=8 * 2 * clips * rows * width,
                transcendentals=pieces * seq * rows // seq,
            ),
        )(*(pltpu.with_memory_space_constraint(x, pltpu.HBM) for x in (q, k, v, dq, dk, dv, gq, gk)))
        out = jax.ShapeDtypeStruct(q.shape, q.dtype)
        return pl.pallas_call(
            write_out,
            out_shape=(out, out),
            in_specs=[pl.BlockSpec(memory_space=pltpu.VMEM)] * 2,
            out_specs=(pl.BlockSpec(memory_space=pl.ANY),) * 2,
            scratch_shapes=[pltpu.SemaphoreType.DMA((2,))],
        )(*(pltpu.with_memory_space_constraint(x, pltpu.VMEM) for x in rows_out))

    shard = P("dp", "seq", None)
    return jax.shard_map(
        on_device,
        mesh=mesh,
        in_specs=(shard,) * 6 + (P("dp"),) * 2,
        out_specs=(shard, shard),
        check_vma=False,
    )
```

```python
import functools

import jax
import jax.numpy as jnp
from jax import lax
from jax.experimental import pallas as pl
from jax.experimental.pallas import tpu as pltpu
from jax.sharding import PartitionSpec as P

EPS = 1e-06
DIM = 128
TILE = 256
MESH = pl.DeviceIdType.MESH
NT = (((1,), (1,)), ((), ()))
V, DV, K, DK, Q, DQ = range(6)


def attend(query, dquery, key, dkey, value, dvalue):
    scale = DIM**-0.5
    scores = lax.dot_general(query, key, NT, preferred_element_type=jnp.float32) * scale
    weights = jnp.exp(scores - jnp.max(scores, axis=-1, keepdims=True))
    weights = weights * (1.0 / jnp.sum(weights, axis=-1, keepdims=True))
    tangent = (
        lax.dot_general(
            jnp.concatenate([dquery, query], 1),
            jnp.concatenate([key, dkey], 1),
            NT,
            preferred_element_type=jnp.float32,
        )
        * scale
    )
    mean = jnp.sum(weights * tangent, axis=-1, keepdims=True)
    low = weights.astype(jnp.bfloat16)
    dlow = (weights * (tangent - mean)).astype(jnp.bfloat16)
    both = jnp.dot(low, jnp.concatenate([value, dvalue], 1), preferred_element_type=jnp.float32)
    dout = jnp.dot(dlow, value, preferred_element_type=jnp.float32) + both[:, DIM:]
    return both[:, :DIM].astype(jnp.bfloat16), dout.astype(jnp.bfloat16)


def write_out(a_ref, b_ref, o_ref, do_ref, sem):
    copies = [
        pltpu.make_async_copy(a_ref, o_ref, sem.at[0]),
        pltpu.make_async_copy(b_ref, do_ref, sem.at[1]),
    ]
    for copy in copies:
        copy.start()
    for copy in copies:
        copy.wait()


def make_kernel(seq, dp, clips, rows, width):
    per_tile = TILE // rows
    plane = 8
    tiles = seq // per_tile

    def kernel(
        q_ref,
        k_ref,
        v_ref,
        dq_ref,
        dk_ref,
        dv_ref,
        gq_ref,
        gk_ref,
        o_ref,
        do_ref,
        normed,
        gathered,
        gains,
        held,
        results,
        load_sem,
        gain_send,
        gain_recv,
        hand_send,
        hand_recv,
        entered,
        send_sem,
        recv_sem,
        back_send,
        back_recv,
        own_sem,
        own_back,
    ):
        me = lax.axis_index("seq")
        group = lax.axis_index("dp")
        row, z = me // plane, me % plane // 2
        half = z // 2

        gates, listeners = ((at * plane + 3, at * plane + 5) for at in (2, 3))

        def is_gate(device):
            return jnp.logical_or(device == gates[0], device == gates[1])

        def is_listener(device):
            return jnp.logical_or(device == listeners[0], device == listeners[1])

        def is_common(device):
            return jnp.logical_not(jnp.logical_or(is_gate(device), is_listener(device)))

        def in_half(r):
            at = lax.rem(row * 4 + me % 4 + r, seq // 2)
            return at // 4 * plane + half * 4 + at % 4

        gate, listener, common = is_gate(me), is_listener(me), is_common(me)
        barrier = pltpu.get_barrier_semaphore()

        def greet(peer):
            pl.semaphore_signal(barrier, inc=1, device_id={"seq": peer}, device_id_type=MESH)

        for peer in listeners:
            pl.when(me != peer)(functools.partial(greet, peer))

        @pl.when(z < 3)
        def _():
            for k in range(4):
                peer = row * plane + (1 - half) * 4 + k
                pl.when(is_common(peer))(functools.partial(greet, peer))

        def greet_dp(r, carry):
            peer = lax.rem(group + r, dp)
            pl.semaphore_signal(barrier, inc=1, device_id={"dp": peer}, device_id_type=MESH)
            return carry

        @pl.when(gate)
        def _():
            lax.fori_loop(1, dp, greet_dp, 0)

        def source(clip, slot, head, early=False):
            columns = pl.ds(pl.multiple_of(head * DIM, DIM), DIM)
            if early:
                return (v_ref, dv_ref)[slot].at[clip, :, columns]
            return normed.at[slot, clip, :, columns]

        def send_one(clip, slot, head, early=False):
            pltpu.make_async_remote_copy(
                src_ref=source(clip, slot, head, early),
                dst_ref=held.at[clip, slot, me],
                send_sem=send_sem.at[clip, slot],
                recv_sem=recv_sem.at[clip, slot],
                device_id={"seq": head},
                device_id_type=MESH,
            ).start()

        def send_early(to):
            for clip in range(clips):
                for slot in (V, DV):
                    for k in range(2):
                        send_one(clip, slot, row * plane + to * 2 + k, early=True)

        @pl.when(jnp.logical_and(common, half == 0))
        def _():
            pl.semaphore_wait(barrier, 2)
            send_early(2)

        @pl.when(jnp.logical_and(common, half == 1))
        def _():
            pl.semaphore_wait(barrier, 4)
            send_early(0)
            send_early(1)

        sources = {V: v_ref, DV: dv_ref, K: k_ref, DK: dk_ref, Q: q_ref, DQ: dq_ref}
        loads = [
            pltpu.make_async_copy(ref, normed.at[slot], load_sem.at[slot])
            for slot, ref in sources.items()
        ]
        for copy in loads:
            copy.start()

        def admit(peer):
            pl.semaphore_signal(entered, inc=1, device_id={"seq": peer}, device_id_type=MESH)

        @pl.when(listener)
        def _():
            pl.semaphore_wait(barrier, seq - 1)

            def tell(r, carry):
                admit(in_half(r))
                return carry

            lax.fori_loop(1, seq // 2, tell, 0)

        @pl.when(jnp.logical_not(listener))
        def _():
            pl.semaphore_wait(entered, 1)

        gain_loads = [
            pltpu.make_async_copy(ref, gathered.at[which, group], load_sem.at[6 + which])
            for which, ref in enumerate((gq_ref, gk_ref))
        ]

        def send_gains():
            for copy in gain_loads:
                copy.start()
            pl.semaphore_wait(barrier, dp - 1)
            for which, ref in enumerate((gq_ref, gk_ref)):

                def send_gain(r, carry):
                    peer = lax.rem(group + r, dp)
                    pltpu.make_async_remote_copy(
                        src_ref=ref,
                        dst_ref=gathered.at[which, group],
                        send_sem=gain_send.at[which],
                        recv_sem=gain_recv.at[which],
                        device_id={"dp": peer},
                        device_id_type=MESH,
                    ).start()
                    return carry

                lax.fori_loop(1, dp, send_gain, 0)

        def hand_gains():
            for which in range(2):
                gain_loads[which].wait()
                other = gathered.at[which, pl.ds(0, dp - 1)]
                pltpu.make_async_copy(other, other, gain_recv.at[which]).wait()

            def hand_on(r, carry):
                pltpu.make_async_remote_copy(
                    src_ref=gathered,
                    dst_ref=gathered,
                    send_sem=hand_send.at[r],
                    recv_sem=hand_recv,
                    device_id={"seq": in_half(r)},
                    device_id_type=MESH,
                ).start()
                return carry

            lax.fori_loop(1, seq // 2, hand_on, 0)

        def send(clip, slot):
            def one(r, carry):
                head = lax.rem(me + r, seq)
                if slot in (V, DV):
                    to = head % plane // 2
                    told = jnp.logical_or(to == 2 - 2 * half, to == 2 - half)
                    sent = jnp.logical_and(common, jnp.logical_and(head // plane == row, told))
                    pl.when(jnp.logical_not(sent))(lambda: send_one(clip, slot, head))
                else:
                    send_one(clip, slot, head)
                return carry

            lax.fori_loop(1, seq, one, 0)
            pltpu.make_async_copy(
                source(clip, slot, me), held.at[clip, slot, me], own_sem.at[clip, slot]
            ).start()

        def others(clip, slot):
            return held.at[clip, slot, pl.ds(0, seq - 1)]

        def arrive(clip, slot):
            pltpu.make_async_copy(
                others(clip, slot), others(clip, slot), recv_sem.at[clip, slot]
            ).wait()
            pltpu.make_async_copy(
                held.at[clip, slot, me], held.at[clip, slot, me], own_sem.at[clip, slot]
            ).wait()

        def normalize(clip, slot, which):
            def step(i, carry):
                part = pl.ds(pl.multiple_of(i * 16, 16), 16)
                x = normed[slot, clip, part, :].astype(jnp.float32)
                dx = normed[slot + 1, clip, part, :].astype(jnp.float32)
                gain = gains[which]
                inverse = lax.rsqrt(jnp.sum(x * x, axis=-1, keepdims=True) * (1.0 / width) + EPS)
                cross = jnp.sum(x * dx, axis=-1, keepdims=True) * (1.0 / width)
                normed[slot, clip, part, :] = (x * inverse * gain).astype(jnp.bfloat16)
                normed[slot + 1, clip, part, :] = (
                    (dx * inverse - x * (inverse * inverse * inverse * cross)) * gain
                ).astype(jnp.bfloat16)
                return carry

            lax.fori_loop(0, rows // 16, step, 0)

        loads[V].wait()
        loads[DV].wait()
        send(0, V)
        pl.when(gate)(send_gains)
        send(0, DV)
        pl.when(gate)(hand_gains)
        for clip in range(1, clips):
            send(clip, V)
            send(clip, DV)

        @pl.when(jnp.logical_not(gate))
        def _():
            pltpu.make_async_copy(gathered, gathered, hand_recv).wait()

        for which in range(2):
            chunks = width // dp // DIM
            for owner in range(dp):
                for j in range(chunks):
                    at = (owner * chunks + j) * DIM
                    gains[which, :, at : at + DIM] = gathered[which, owner, j : j + 1, :]
        for copy in loads[K:]:
            copy.wait()

        normalize(0, K, 1)
        send(0, K)
        send(0, DK)
        normalize(0, Q, 0)
        for clip in range(1, clips):
            normalize(clip, K, 1)
            normalize(clip, Q, 0)

        def tile_of(i):
            crosses, k = i % 2, i // 2
            outer = 1 - (row + 1) // 2 % 2
            served = k + (1 - outer) * (1 - 2 * (k % 2))
            near = lax.rem(row + k + 1, tiles // 2)
            return (crosses * served + (1 - crosses) * near) * 2 + (half + crosses) % 2

        def compute(clip, i):
            first = tile_of(i) * per_tile
            took = pl.ds(first, per_tile)

            def whole(slot):
                return held[clip, slot].reshape(seq * rows, DIM)

            out, dout = attend(
                held[clip, Q, took].reshape(TILE, DIM),
                held[clip, DQ, took].reshape(TILE, DIM),
                whole(K),
                whole(DK),
                whole(V),
                whole(DV),
            )
            results[clip, 0, took] = out.reshape(per_tile, rows, DIM)
            results[clip, 1, took] = dout.reshape(per_tile, rows, DIM)

        mine = pl.ds(pl.multiple_of(me * DIM, DIM), DIM)

        def give_back(clip, which, i, pieces=range(per_tile)):
            ref = (o_ref, do_ref)[which]
            first = tile_of(i) * per_tile
            for r in pieces:
                token = first + half * r + (1 - half) * (per_tile - 1 - r)

                @pl.when(token != me)
                def _():
                    pltpu.make_async_remote_copy(
                        src_ref=results.at[clip, which, token],
                        dst_ref=ref.at[clip, :, mine],
                        send_sem=back_send.at[clip, which],
                        recv_sem=back_recv.at[clip, which],
                        device_id={"seq": token},
                        device_id_type=MESH,
                    ).start()

                @pl.when(token == me)
                def _():
                    pltpu.make_async_copy(
                        results.at[clip, which, token],
                        ref.at[clip, :, mine],
                        own_back.at[clip, which],
                    ).start()

        def loop(low, high, body):
            def step(i, carry):
                body(i)
                return carry

            lax.fori_loop(low, high, step, 0)

        arrive(0, V)
        send(0, Q)
        arrive(0, DV)
        send(0, DQ)
        arrive(1, V)
        send(1, K)
        arrive(1, DV)
        send(1, DK)
        arrive(0, K)
        send(1, Q)
        arrive(0, DK)
        send(1, DQ)
        arrive(0, Q)
        arrive(0, DQ)
        loop(0, tiles, lambda i: compute(0, i))
        arrive(1, K)
        arrive(1, DK)
        loop(0, tiles, lambda i: give_back(0, 0, i))
        arrive(1, Q)
        arrive(1, DQ)
        loop(0, tiles, lambda i: give_back(0, 1, i))

        def last(i):
            compute(1, i)
            for which in range(2):
                give_back(1, which, i, range(per_tile // 2))

            @pl.when(jnp.logical_or(half == 0, i % 2 == 0))
            def _():
                for which in range(2):
                    give_back(1, which, i, range(per_tile // 2, per_tile))

        loop(0, tiles, last)

        @pl.when(half == 1)
        def _():
            def rest(i):
                for which in range(2):
                    give_back(1, which, 2 * i + 1, range(per_tile // 2, per_tile))

            loop(0, tiles // 2, rest)

        @pl.when(gate)
        def _():
            for which in range(2):
                other = gathered.at[which, pl.ds(0, dp - 1)]
                pltpu.make_async_copy(other, other, gain_send.at[which]).wait()

            def handed(r, carry):
                pltpu.make_async_copy(gathered, gathered, hand_send.at[r]).wait()
                return carry

            lax.fori_loop(1, seq // 2, handed, 0)

        for clip in range(clips):
            for slot in range(6):
                pltpu.make_async_copy(
                    others(clip, slot), others(clip, slot), send_sem.at[clip, slot]
                ).wait()
            for which in range(2):
                own, some = results.at[clip, which, 0], results.at[clip, which, pl.ds(0, seq - 1)]
                pltpu.make_async_copy(some, some, back_send.at[clip, which]).wait()
                pltpu.make_async_copy(own, own, own_back.at[clip, which]).wait()
                pltpu.make_async_copy(some, some, back_recv.at[clip, which]).wait()

    return kernel


def solution(mesh):
    seq, dp = mesh.shape["seq"], mesh.shape["dp"]

    def on_device(q, k, v, dq, dk, dv, gq, gk):
        clips, rows, width = q.shape
        gq, gk = (gain.reshape(gain.shape[0] // DIM, DIM) for gain in (gq, gk))
        pieces = clips * seq * seq * rows
        rows_out = pl.pallas_call(
            make_kernel(seq, dp, clips, rows, width),
            out_shape=(pltpu.VMEM(q.shape, q.dtype),) * 2,
            in_specs=[pl.BlockSpec(memory_space=pl.ANY)] * 8,
            out_specs=(pl.BlockSpec(memory_space=pltpu.VMEM),) * 2,
            scratch_shapes=[
                pltpu.VMEM((6, clips, rows, width), jnp.bfloat16),
                pltpu.VMEM((2, dp) + gq.shape, jnp.float32),
                pltpu.VMEM((2, 1, width), jnp.float32),
                pltpu.VMEM((clips, 6, seq, rows, DIM), jnp.bfloat16),
                pltpu.VMEM((clips, 2, seq, rows, DIM), jnp.bfloat16),
                pltpu.SemaphoreType.DMA((8,)),
                pltpu.SemaphoreType.DMA((2,)),
                pltpu.SemaphoreType.DMA((2,)),
                pltpu.SemaphoreType.DMA((seq // 2,)),
                pltpu.SemaphoreType.DMA,
                pltpu.SemaphoreType.REGULAR,
                pltpu.SemaphoreType.DMA((clips, 6)),
                pltpu.SemaphoreType.DMA((clips, 6)),
                pltpu.SemaphoreType.DMA((clips, 2)),
                pltpu.SemaphoreType.DMA((clips, 2)),
                pltpu.SemaphoreType.DMA((clips, 6)),
                pltpu.SemaphoreType.DMA((clips, 2)),
            ],
            compiler_params=pltpu.CompilerParams(
                collective_id=0, has_side_effects=True, vmem_limit_bytes=48 * 2**20
            ),
            cost_estimate=pl.CostEstimate(
                flops=12 * pieces * seq * rows * DIM // seq,
                bytes_accessed=8 * 2 * clips * rows * width,
                transcendentals=pieces * seq * rows // seq,
            ),
        )(*(pltpu.with_memory_space_constraint(x, pltpu.HBM) for x in (q, k, v, dq, dk, dv, gq, gk)))
        out = jax.ShapeDtypeStruct(q.shape, q.dtype)
        return pl.pallas_call(
            write_out,
            out_shape=(out, out),
            in_specs=[pl.BlockSpec(memory_space=pltpu.VMEM)] * 2,
            out_specs=(pl.BlockSpec(memory_space=pl.ANY),) * 2,
            scratch_shapes=[pltpu.SemaphoreType.DMA((2,))],
        )(*(pltpu.with_memory_space_constraint(x, pltpu.VMEM) for x in rows_out))

    shard = P("dp", "seq", None)
    return jax.shard_map(
        on_device,
        mesh=mesh,
        in_specs=(shard,) * 6 + (P("dp"),) * 2,
        out_specs=(shard, shard),
        check_vma=False,
    )
```
